256 devices in a mesh: blk: 64 (over z, y, core), smp: 4 (over x).
Axes of the slice: x: 4, y: 4, z: 8, core: 2. Of those that a mesh axis runs over, the one named last changes fastest.
Arguments:
- forward_samples: bfloat16 [256, 524288], P('smp', 'blk'), may hold values from -0.375 to 0.375
- adjoint_samples: bfloat16 [256, 131072], P('smp', 'blk'), may hold values from -0.125 to 0.125
- probe_values: bfloat16 [131072, 192], P('blk'), may hold values from -6 to 6
- owners: int32 [131072, 1], P('blk'), may hold values from 0 to 63; in each aligned block of 2048 rows (0 to 2047, 2048 to 4095, ...) at most 64 rows name the same one
- block_ranks: int32 [64], P('blk'), may hold values from 64 to 256
- twiddle: float32 [2, 524288], P(None, 'blk'), may hold values from -1.2 to 1.2
Outputs:
- applied: bfloat16 [192, 524288], P('smp', 'blk')
The draws below stay inside these ranges and needn't reach their ends.
Inputs may be any that keep to these rules, and one draw needn't show every extreme that they name: `owners`: in the rows of one block index no owner block is named more than 64 times.
All inputs are finite; a program needn't handle non-finite values.
Results may differ from the reference program's by a relative error of at most 0.005.
Values may be sent and summed in bfloat16 or wider, within the bound.
No kernel may reach another device: no remote copies, remote signals or barrier semaphores. Data moves between devices by JAX's collectives and lax.ppermute only.
A program may use at most 64 MiB of HBM per device.

```python
import math
import jax
import jax.numpy as jnp
import numpy as np
from jax import lax

SAMPLES = 256
BOX = 8192
VECTORS = 192
ADJ_ROWS = 2048
LEVELS = 2
BLOCKS = 64
CAPACITY = 64
N_BLK = 64


def with_ends(array, own_key, smallest, largest):
    spot = [jax.random.randint(jax.random.fold_in(own_key, axis), (), 0, length) for axis, length in enumerate(array.shape)]
    longest = array.shape.index(max(array.shape))
    beside = spot[:longest] + [(spot[longest] + 1) % array.shape[longest]] + spot[longest + 1:]
    return array.at[tuple(spot)].set(smallest).at[tuple(beside)].set(largest)


def block_levels(rng, shape, pieces, least, high):
    loudness, own = 1.0, jax.random.fold_in(rng, 6)
    for position, parts in pieces:
        steps = jnp.exp(jax.random.uniform(jax.random.fold_in(own, position), (parts,), jnp.float32, least / len(pieces), high / len(pieces)))
        loudness = loudness * jnp.repeat(steps, shape[position] // parts).reshape([-1 if axis == position else 1 for axis in range(len(shape))])
    return loudness


def shared_out(key, own, number, rows, amount, top, limit, lean):
    ranking = jax.random.permutation(key, amount)
    crowded, common = load_shares(amount, rows * top, limit, lean, True), load_shares(amount, rows * top, limit, lean, False)
    places = jnp.arange(amount)

    def named(lengths, rotation):
        used = int((lengths > 0).sum())
        fixed = max(1, used // 4)
        moved = fixed + (places - fixed + rotation * (used - fixed)) % max(1, amount - fixed)
        return jnp.zeros((amount,), jnp.int32).at[ranking[jnp.where(places < fixed, places, moved)]].set(jnp.asarray(lengths, jnp.int32))

    lengths = jnp.where(number % 4 == 0, named(crowded, number // 4), named(common, number - number // 4 - 1))
    mixed = jax.random.permutation(jax.random.fold_in(own, 3), amount)
    source_of, sink = mixed[0:amount // 2 * 2:2], mixed[1:amount // 2 * 2:2]
    margin = jnp.minimum(lengths[source_of] - 1, limit - lengths[sink]) // 2
    margin = jnp.where((source_of == ranking[0]) | (sink == ranking[0]) | (lengths[sink] == 0), 0, jnp.maximum(margin, 0))
    moved = jax.random.randint(jax.random.fold_in(own, 4), (amount // 2,), 0, 1 << 20) % (margin + 1)
    lengths = lengths.at[source_of].add(-moved).at[sink].add(moved)
    members = jnp.searchsorted(jnp.cumsum(lengths), jnp.arange(rows * top), side="right").astype(jnp.int32)
    listing = members.reshape(top, rows).T
    listing = listing[jax.random.permutation(jax.random.fold_in(own, 1), rows)]
    rotation = jax.random.randint(jax.random.fold_in(own, 2), (rows, 1), 0, top)
    return jnp.take_along_axis(listing, (jnp.arange(top)[None, :] + rotation) % top, axis=1)


def load_shares(amount, total, reach, lean, full):
    weights = [(1 << 20) // math.isqrt(grade ** lean) + 1 for grade in range(1, amount + 1)]
    largest = reach if full else min(reach, max(-(-total // amount), total * weights[0] // sum(weights)))
    least = 1 if total - largest >= amount - 1 else 0
    holding, spare = [largest] + [least] * (amount - 1), total - largest - least * (amount - 1)
    while spare > 0:
        movable = [i for i in range(1, amount) if holding[i] < largest] or [i for i in range(1, amount) if holding[i] < reach]
        mass, budget = sum([weights[i] for i in movable]), spare
        for i in movable:
            extra = min(reach - holding[i], max(1, budget * weights[i] // mass), spare)
            holding[i] = holding[i] + extra
            spare = spare - extra
    return np.array(holding)


def gaussian(key, shape, scale, reach, cuts=(), kind=jnp.bfloat16):
    values = jax.random.normal(key, shape, jnp.float32) * scale
    if len(cuts) > 0:
        values = block_levels(key, shape, cuts, -0.22, 0.18) * values
    return jnp.clip(values, min=-reach, max=reach).astype(kind)


def setup_inputs(seed: int = 0) -> dict:
    streams_of = jax.random.split(jax.random.key(seed), 7)
    forward_samples = gaussian(streams_of[0], (SAMPLES, BLOCKS * BOX), SAMPLES ** -0.5, 0.375, ((0, 4), (1, 64)))
    adjoint_samples = gaussian(streams_of[1], (SAMPLES, BLOCKS * ADJ_ROWS), ADJ_ROWS ** -0.5, 0.125, ((0, 4), (1, 64)))
    probe_values = gaussian(streams_of[2], (BLOCKS * ADJ_ROWS, VECTORS), 1.0, 6.0, ((0, 64),))
    owners_keys = jax.random.split(jax.random.fold_in(streams_of[3], 1), (BLOCKS * ADJ_ROWS) // ADJ_ROWS)
    owners_turns = jax.random.permutation(jax.random.fold_in(streams_of[3], 3), (BLOCKS * ADJ_ROWS) // ADJ_ROWS)
    owners = jax.vmap(lambda own, number: shared_out(jax.random.fold_in(streams_of[3], 2), own, number, ADJ_ROWS, BLOCKS, 1, CAPACITY, 2))(owners_keys, owners_turns).reshape((BLOCKS * ADJ_ROWS, 1))
    block_ranks = with_ends(jax.random.randint(streams_of[4], (BLOCKS,), SAMPLES // 4, SAMPLES + 1), jax.random.fold_in(streams_of[4], 1), SAMPLES // 4, SAMPLES).astype(jnp.int32)
    twiddle = jnp.clip(jax.random.uniform(streams_of[5], (LEVELS, BLOCKS * BOX), jnp.float32, -1.2, 1.2) * block_levels(streams_of[5], (LEVELS, BLOCKS * BOX), ((1, 64),), -0.4, 0.0), -1.2, 1.2)
    return dict(forward_samples=forward_samples, adjoint_samples=adjoint_samples, probe_values=probe_values, owners=owners, block_ranks=block_ranks, twiddle=twiddle)


def reference(forward_samples, adjoint_samples, probe_values, owners, block_ranks, twiddle):
    blocks = N_BLK
    owner_ids = owners[:, 0].astype(jnp.int32)
    per_block = ADJ_ROWS
    adj_rows = adjoint_samples.astype(jnp.float32).T.reshape(blocks, per_block, SAMPLES)
    probe_rows = probe_values.astype(jnp.float32).reshape(blocks, per_block, VECTORS)
    owner_rows = owner_ids.reshape(blocks, per_block)

    def accumulate(carry, items):
        adj_part, probe_part, owner_part = items
        outer = adj_part[:, :, None] * probe_part[:, None, :]
        return carry + jax.ops.segment_sum(outer, owner_part, num_segments=blocks), None

    start_sum = jnp.zeros((blocks, SAMPLES, VECTORS), jnp.float32)
    coeffs, unused = lax.scan(accumulate, start_sum, (adj_rows, probe_rows, owner_rows))
    keep_mask = (jnp.arange(SAMPLES, dtype=jnp.int32)[None, :] < block_ranks[:, None]).astype(jnp.float32)
    weights = lax.optimization_barrier((coeffs * keep_mask[:, :, None]).astype(jnp.bfloat16)).astype(jnp.float32)
    forward_grid = forward_samples.astype(jnp.float32).reshape(SAMPLES, blocks, BOX)
    field = jnp.einsum('bsv,sbm->vbm', weights, forward_grid)
    factors = twiddle.astype(jnp.float32).reshape(LEVELS, blocks, BOX)
    for level_index in range(LEVELS):
        distance = blocks // (2 ** (level_index + 1))
        partner_ids = jnp.bitwise_xor(jnp.arange(blocks, dtype=jnp.int32), distance)
        partner = jnp.take(field, partner_ids, axis=1)
        field = field + factors[level_index][None, :, :] * partner
    return field.reshape(VECTORS, blocks * BOX).astype(jnp.bfloat16)
```

```python
import functools

import jax
import jax.numpy as jnp
from jax import lax
from jax.experimental import pallas as pl
from jax.experimental.pallas import tpu as pltpu
from jax.sharding import Mesh, PartitionSpec as P

GROUP = ("zg", "smp")
Z_AXES = ("zg", "zl")
BLK = ("zg", "zl", "y", "core")
STEP = 8


def partial_kernel(parity_ref, owners_ref, adjoint_ref, probes_ref, out_ref, masked, wide):
    step = pl.program_id(0)
    samples = adjoint_ref.shape[0]
    vectors = probes_ref.shape[0]

    @pl.when(step == 0)
    def _():
        wide[:vectors, :] = probes_ref[...]
        wide[vectors:, :] = probes_ref[128:, :]

    own = owners_ref[...]
    adjoint = adjoint_ref[...]
    y_count = pl.num_programs(0)
    for z in range(STEP):
        owner = (z * y_count + step) * 2 + parity_ref[0]
        hot = jnp.where(own == owner, 1.0, 0.0).astype(jnp.bfloat16)
        masked[z * samples:(z + 1) * samples, :] = adjoint * hot
    product = lax.dot_general(
        masked[...], wide[...], (((1,), (1,)), ((), ())), preferred_element_type=jnp.float32
    )
    half = samples // 2
    low = lax.broadcasted_iota(jnp.int32, (half, 128), 1) < 64
    for z in range(STEP):
        block = product[z * samples:(z + 1) * samples, :]
        out_ref[0, z, :samples, :] = block[:, :128]
        out_ref[0, z, samples:, :] = jnp.where(low, block[:half, 128:], block[half:, 128:])


def partial_coeffs(parity, owners, adjoint, probes):
    samples, rows = adjoint.shape
    vectors = probes.shape[0]
    y_count = lax.axis_size("y")
    packed = samples * vectors // 128
    return pl.pallas_call(
        partial_kernel,
        grid=(y_count,),
        in_specs=[
            pl.BlockSpec(memory_space=pltpu.SMEM),
            pl.BlockSpec((1, rows), lambda i: (0, 0)),
            pl.BlockSpec((samples, rows), lambda i: (0, 0)),
            pl.BlockSpec((vectors, rows), lambda i: (0, 0)),
        ],
        out_specs=pl.BlockSpec((1, STEP, packed, 128), lambda i: (i, 0, 0, 0)),
        out_shape=jax.ShapeDtypeStruct((y_count, STEP, packed, 128), jnp.float32),
        scratch_shapes=[
            pltpu.VMEM((STEP * samples, rows), jnp.bfloat16),
            pltpu.VMEM((256, rows), jnp.bfloat16),
        ],
        compiler_params=pltpu.CompilerParams(vmem_limit_bytes=24 * 1024 * 1024),
        cost_estimate=pl.CostEstimate(
            flops=2 * y_count * STEP * samples * rows * 256,
            bytes_accessed=3 * 1024 * 1024,
            transcendentals=0,
        ),
    )(parity, owners, adjoint, probes)


def field_kernel(weights_ref, samples_ref, twiddle_ref, out_ref, field):
    blocks = twiddle_ref.shape[0]
    parts = weights_ref.shape[0] // blocks
    samples = samples_ref.shape[1]
    half = samples // 2
    vectors = field.shape[1]
    for c in range(blocks):
        grid = samples_ref[c * parts:(c + 1) * parts].reshape(parts * samples, -1)
        head = [weights_ref[c * parts + p, :samples, :] for p in range(parts)]
        tail = []
        for p in range(parts):
            rest = weights_ref[c * parts + p, samples:, :]
            tail += [rest[:, :64], rest[:, 64:]]
        head = jnp.concatenate(head, axis=0)
        tail = jnp.concatenate(tail, axis=0)
        field[c, :128, :] = lax.dot_general(
            head, grid, (((0,), (0,)), ((), ())), preferred_element_type=jnp.float32
        )
        field[c, 128:, :] = lax.dot_general(
            tail, grid, (((0,), (0,)), ((), ())), preferred_element_type=jnp.float32
        )
    share = vectors // parts
    for p in range(parts):
        rows = slice(p * share, (p + 1) * share)
        level = [field[c, rows, :] for c in range(blocks)]
        for index, distance in enumerate((2, 1)):
            level = [
                level[c] + twiddle_ref[c, index:index + 1, :] * level[c ^ distance]
                for c in range(blocks)
            ]
        for c in range(blocks):
            out_ref[c * parts + p] = level[c].astype(jnp.bfloat16)


def butterfly(weights, samples, twiddle, vectors):
    pieces, _, points = samples.shape
    share = vectors * twiddle.shape[0] // pieces
    return pl.pallas_call(
        field_kernel,
        out_shape=jax.ShapeDtypeStruct((pieces, share, points), jnp.bfloat16),
        in_specs=[pl.BlockSpec(memory_space=pltpu.VMEM)] * 3,
        out_specs=pl.BlockSpec(memory_space=pltpu.VMEM),
        scratch_shapes=[pltpu.VMEM((twiddle.shape[0], vectors, points), jnp.float32)],
        compiler_params=pltpu.CompilerParams(vmem_limit_bytes=24 * 1024 * 1024),
        cost_estimate=pl.CostEstimate(
            flops=2 * pieces * 64 * vectors * points,
            bytes_accessed=3 * 1024 * 1024,
            transcendentals=0,
        ),
    )(weights, samples, twiddle)


def body(forward_samples, adjoint_samples, probe_values, owners, block_ranks, twiddle):
    groups = lax.axis_size("zg")
    parts = lax.axis_size("smp")
    samples, points = forward_samples.shape
    vectors = probe_values.shape[1]
    members = groups * parts
    smp = lax.axis_index("smp")
    core = lax.axis_index("core")

    pieces = forward_samples.reshape(samples, members, points // members).transpose(1, 0, 2)
    pieces = lax.all_to_all(pieces, GROUP, 0, 0, tiled=True)
    factors = twiddle.reshape(twiddle.shape[0], groups, parts, points // members)
    factors = lax.dynamic_index_in_dim(factors, smp, 2, keepdims=False).transpose(1, 0, 2)
    factors = lax.all_to_all(factors, "zg", 0, 0, tiled=True)

    own, probes = owners.T, probe_values.T
    sent = partial_coeffs((1 - core)[None], own, adjoint_samples, probes)
    came = lax.ppermute(sent, "core", [(0, 1), (1, 0)])
    kept = partial_coeffs(core[None], own, adjoint_samples, probes)
    sums = (kept + came).astype(jnp.bfloat16)
    sums = lax.all_to_all(sums, "y", 0, 0, tiled=True)
    sums = jnp.sum(sums.astype(jnp.float32), axis=0).astype(jnp.bfloat16)
    sums = lax.all_to_all(sums, Z_AXES, 0, 0, tiled=True)
    coeffs = jnp.sum(sums.astype(jnp.float32), axis=0)

    row = lax.broadcasted_iota(jnp.int32, coeffs.shape, 0)
    lane = lax.broadcasted_iota(jnp.int32, coeffs.shape, 1)
    tail = row - samples + jnp.where(lane < 64, 0, samples // 2)
    sample = smp * samples + jnp.where(row < samples, row, tail)
    weights = jnp.where(sample < block_ranks[0], coeffs, 0.0).astype(jnp.bfloat16)
    weights = jnp.broadcast_to(weights[None], (members,) + weights.shape)
    weights = lax.all_to_all(weights, GROUP, 0, 0, tiled=True)

    result = butterfly(weights, pieces, factors, vectors)
    result = lax.all_to_all(result, GROUP, 0, 0, tiled=True)
    return result.transpose(1, 0, 2).reshape(vectors // parts, points)


def solution(mesh):
    grid = Mesh(mesh.devices.reshape(4, 2, 4, 2, 4), BLK + ("smp",))
    in_specs = (
        P("smp", BLK),
        P("smp", BLK),
        P(BLK, None),
        P(BLK, None),
        P(BLK),
        P(None, BLK),
    )
    out_specs = P("smp", BLK)
    return jax.shard_map(body, mesh=grid, in_specs=in_specs, out_specs=out_specs, check_vma=False)
```

```python
import jax
import jax.numpy as jnp
from jax import lax
from jax.experimental import pallas as pl
from jax.experimental.pallas import tpu as pltpu
from jax.sharding import Mesh, PartitionSpec as P

GROUP = ("zg", "smp")
Z_AXES = ("zg", "zl")
BLK = ("zg", "zl", "y", "core")
MIB = 1024 * 1024
VMEM = pl.BlockSpec(memory_space=pltpu.VMEM)
SMEM = pl.BlockSpec(memory_space=pltpu.SMEM)


def partial_kernel(place_ref, owners_ref, adjoint_ref, probes_ref, out_ref, masked, wide):
    step = pl.program_id(0)
    y_count = pl.num_programs(0)
    z_count = out_ref.shape[1]
    samples = adjoint_ref.shape[0]
    vectors = probes_ref.shape[0]

    @pl.when(step == 0)
    def _():
        wide[:vectors, :] = probes_ref[...]
        wide[vectors:, :] = probes_ref[128:, :]

    own = owners_ref[...]
    adjoint = adjoint_ref[...]
    y = lax.rem(place_ref[1] + step, y_count)
    for offset in range(z_count):
        z = lax.rem(place_ref[0] + offset, z_count)
        owner = (z * y_count + y) * 2 + place_ref[2]
        hot = jnp.where(own == owner, 1.0, 0.0).astype(jnp.bfloat16)
        masked[offset * samples:(offset + 1) * samples, :] = adjoint * hot
    product = lax.dot_general(
        masked[...], wide[...], (((1,), (1,)), ((), ())), preferred_element_type=jnp.float32
    )
    half = samples // 2
    low = lax.broadcasted_iota(jnp.int32, (half, 128), 1) < 64
    for offset in range(z_count):
        block = product[offset * samples:(offset + 1) * samples, :]
        out_ref[0, offset, :samples, :] = block[:, :128]
        out_ref[0, offset, samples:, :] = jnp.where(low, block[:half, 128:], block[half:, 128:])


def partial_coeffs(place, owners, adjoint, probes):
    samples, rows = adjoint.shape
    vectors = probes.shape[0]
    y_count, z_count = lax.axis_size("y"), lax.axis_size(Z_AXES)
    packed = samples * vectors // 128
    return pl.pallas_call(
        partial_kernel,
        grid=(y_count,),
        in_specs=[
            SMEM,
            pl.BlockSpec((1, rows), lambda i: (0, 0)),
            pl.BlockSpec((samples, rows), lambda i: (0, 0)),
            pl.BlockSpec((vectors, rows), lambda i: (0, 0)),
        ],
        out_specs=pl.BlockSpec((1, z_count, packed, 128), lambda i: (i, 0, 0, 0)),
        out_shape=jax.ShapeDtypeStruct((y_count, z_count, packed, 128), jnp.float32),
        scratch_shapes=[
            pltpu.VMEM((z_count * samples, rows), jnp.bfloat16),
            pltpu.VMEM((256, rows), jnp.bfloat16),
        ],
        compiler_params=pltpu.CompilerParams(vmem_limit_bytes=24 * MIB),
        cost_estimate=pl.CostEstimate(
            flops=2 * y_count * z_count * samples * rows * 256,
            bytes_accessed=3 * MIB,
            transcendentals=0,
        ),
    )(place, owners, adjoint, probes)


def local_call(kernel, out_shape, *args, smem=0, scratch=(), flops=0):
    return pl.pallas_call(
        kernel,
        out_shape=out_shape,
        in_specs=[SMEM] * smem + [VMEM] * (len(args) - smem),
        out_specs=jax.tree.map(lambda _: VMEM, out_shape),
        scratch_shapes=list(scratch),
        compiler_params=pltpu.CompilerParams(vmem_limit_bytes=24 * MIB),
        cost_estimate=pl.CostEstimate(flops=flops, bytes_accessed=2 * MIB, transcendentals=0),
    )(*args)


def merge_kernel(kept_ref, came_ref, own_ref, *out_refs):
    own_ref[...] = kept_ref[0] + came_ref[0]
    for offset, out_ref in enumerate(out_refs, 1):
        out_ref[...] = (kept_ref[offset] + came_ref[offset]).astype(out_ref.dtype)


def spread_kernel(count, *refs):
    total = refs[0][...]
    for ref in refs[1:count]:
        total = total + ref[...].astype(jnp.float32)
    for offset, out_ref in enumerate(refs[count:]):
        out_ref[...] = total[offset].astype(out_ref.dtype)


def weights_kernel(place_ref, *refs):
    total = refs[0][...]
    for ref in refs[1:-1]:
        total = total + ref[...].astype(jnp.float32)
    samples = total.shape[0] * 2 // 3
    row = lax.broadcasted_iota(jnp.int32, total.shape, 0)
    lane = lax.broadcasted_iota(jnp.int32, total.shape, 1)
    tail = row - samples + jnp.where(lane < 64, 0, samples // 2)
    sample = place_ref[0] * samples + jnp.where(row < samples, row, tail)
    refs[-1][...] = jnp.where(sample < place_ref[1], total, 0.0).astype(jnp.bfloat16)


def field_kernel(blocks, parts, place_ref, samples_ref, *refs):
    twiddle_refs, weight_refs = refs[:blocks], refs[blocks:-2]
    out_ref, field = refs[-2:]
    zg, smp = place_ref[0], place_ref[1]
    samples, points = samples_ref.shape[1:]
    vectors = field.shape[1]
    for c in range(blocks):
        block = zg ^ c
        grid, head, tail = [], [], []
        for p in range(parts):
            grid.append(samples_ref[block * parts + lax.rem(smp - p + parts, parts)])
            weights = weight_refs[c * parts + p]
            head.append(weights[:samples, :])
            rest = weights[samples:, :]
            tail += [rest[:, :64], rest[:, 64:]]
        grid = jnp.concatenate(grid, axis=0)
        head = jnp.concatenate(head, axis=0)
        tail = jnp.concatenate(tail, axis=0)
        field[c, :128, :] = lax.dot_general(
            head, grid, (((0,), (0,)), ((), ())), preferred_element_type=jnp.float32
        )
        field[c, 128:, :] = lax.dot_general(
            tail, grid, (((0,), (0,)), ((), ())), preferred_element_type=jnp.float32
        )
    share = vectors // parts
    for p in range(parts):
        rows = slice(p * share, (p + 1) * share)
        level = [field[c, rows, :] for c in range(blocks)]
        for index, distance in enumerate((2, 1)):
            level = [
                level[c] + twiddle_refs[c][index:index + 1, :] * level[c ^ distance]
                for c in range(blocks)
            ]
        for c in range(blocks):
            out_ref[(zg ^ c) * parts + p] = level[c].astype(jnp.bfloat16)


def turn(x, axis, offset):
    count = lax.axis_size(axis)
    return lax.ppermute(x, axis, [(i, (i + offset) % count) for i in range(count)])


def body(forward_samples, adjoint_samples, probe_values, owners, block_ranks, twiddle):
    groups, parts = lax.axis_size("zg"), lax.axis_size("smp")
    y_count, z_count = lax.axis_size("y"), lax.axis_size(Z_AXES)
    samples, points = forward_samples.shape
    vectors = probe_values.shape[1]
    members = groups * parts
    piece = points // members
    zg, smp = lax.axis_index("zg"), lax.axis_index("smp")
    z, y, core = lax.axis_index(Z_AXES), lax.axis_index("y"), lax.axis_index("core")

    pieces = forward_samples.reshape(samples, members, piece).transpose(1, 0, 2)
    pieces = lax.all_to_all(pieces, GROUP, 0, 0, tiled=True)
    factors = []
    for c in range(groups):
        start = ((zg ^ c) * parts + smp) * piece
        part = lax.dynamic_slice_in_dim(twiddle, start, piece, 1)
        factors.append(lax.ppermute(part, "zg", [(i, i ^ c) for i in range(groups)]) if c else part)

    own, probes = owners.T, probe_values.T
    sent = partial_coeffs(jnp.stack([z, y, 1 - core]), own, adjoint_samples, probes)
    came = lax.ppermute(sent, "core", [(0, 1), (1, 0)])
    kept = partial_coeffs(jnp.stack([z, y, core]), own, adjoint_samples, probes)
    packed = kept.shape[2:]
    shapes = [jax.ShapeDtypeStruct((z_count,) + packed, jnp.float32)]
    shapes += [jax.ShapeDtypeStruct((z_count,) + packed, jnp.bfloat16)] * (y_count - 1)
    sums = local_call(merge_kernel, shapes, kept, came)
    sums = [sums[0]] + [turn(sums[i], "y", i) for i in range(1, y_count)]
    shapes = [jax.ShapeDtypeStruct(packed, jnp.float32)]
    shapes += [jax.ShapeDtypeStruct(packed, jnp.bfloat16)] * (z_count - 1)
    sums = local_call(lambda *refs: spread_kernel(y_count, *refs), shapes, *sums)
    sums = [sums[0]] + [turn(sums[i], Z_AXES, i) for i in range(1, z_count)]
    weights = local_call(
        weights_kernel,
        jax.ShapeDtypeStruct(packed, jnp.bfloat16),
        jnp.stack([smp, block_ranks[0]]),
        *sums,
        smem=1,
    )
    every = []
    for c in range(groups):
        for p in range(parts):
            route = [
                (i, (i // parts ^ c) * parts + (i + p) % parts) for i in range(members)
            ]
            every.append(lax.ppermute(weights, GROUP, route) if c or p else weights)

    result = local_call(
        lambda *refs: field_kernel(groups, parts, *refs),
        jax.ShapeDtypeStruct((members, vectors // parts, piece), jnp.bfloat16),
        jnp.stack([zg, smp]),
        pieces,
        *factors,
        *every,
        smem=1,
        scratch=[pltpu.VMEM((groups, vectors, piece), jnp.float32)],
        flops=2 * members * samples * vectors * piece,
    )
    result = lax.all_to_all(result, GROUP, 0, 0, tiled=True)
    return result.transpose(1, 0, 2).reshape(vectors // parts, points)


def solution(mesh):
    grid = Mesh(mesh.devices.reshape(4, 2, 4, 2, 4), BLK + ("smp",))
    in_specs = (
        P("smp", BLK),
        P("smp", BLK),
        P(BLK, None),
        P(BLK, None),
        P(BLK),
        P(None, BLK),
    )
    out_specs = P("smp", BLK)
    return jax.shard_map(body, mesh=grid, in_specs=in_specs, out_specs=out_specs, check_vma=False)
```

```python
import jax
import jax.numpy as jnp
from jax import lax
from jax.experimental import pallas as pl
from jax.experimental.pallas import tpu as pltpu
from jax.sharding import Mesh, PartitionSpec as P

GROUP = ("zg", "smp")
Z_AXES = ("zg", "zl")
BLK = ("zg", "zl", "y", "core")
MIB = 1024 * 1024
VMEM = pl.BlockSpec(memory_space=pltpu.VMEM)
SMEM = pl.BlockSpec(memory_space=pltpu.SMEM)


def partial_kernel(place_ref, owners_ref, adjoint_ref, probes_ref, out_ref, masked, wide):
    step = pl.program_id(0)
    y_count = pl.num_programs(0)
    z_count = out_ref.shape[1]
    samples = adjoint_ref.shape[0]
    vectors = probes_ref.shape[0]

    @pl.when(step == 0)
    def _():
        wide[:vectors, :] = probes_ref[...]
        wide[vectors:, :] = probes_ref[128:, :]

    own = owners_ref[...]
    adjoint = adjoint_ref[...]
    y = lax.rem(place_ref[0] + step, y_count)
    for offset in range(z_count):
        owner = (offset * y_count + y) * 2 + place_ref[1]
        hot = jnp.where(own == owner, 1.0, 0.0).astype(jnp.bfloat16)
        masked[offset * samples:(offset + 1) * samples, :] = adjoint * hot
    product = lax.dot_general(
        masked[...], wide[...], (((1,), (1,)), ((), ())), preferred_element_type=jnp.float32
    )
    half = samples // 2
    low = lax.broadcasted_iota(jnp.int32, (half, 128), 1) < 64
    for offset in range(z_count):
        block = product[offset * samples:(offset + 1) * samples, :]
        out_ref[0, offset, :samples, :] = block[:, :128]
        out_ref[0, offset, samples:, :] = jnp.where(low, block[:half, 128:], block[half:, 128:])


def partial_coeffs(place, owners, adjoint, probes):
    samples, rows = adjoint.shape
    vectors = probes.shape[0]
    y_count, z_count = lax.axis_size("y"), lax.axis_size(Z_AXES)
    packed = samples * vectors // 128
    return pl.pallas_call(
        partial_kernel,
        grid=(y_count,),
        in_specs=[
            SMEM,
            pl.BlockSpec((1, rows), lambda i: (0, 0)),
            pl.BlockSpec((samples, rows), lambda i: (0, 0)),
            pl.BlockSpec((vectors, rows), lambda i: (0, 0)),
        ],
        out_specs=pl.BlockSpec((1, z_count, packed, 128), lambda i: (i, 0, 0, 0)),
        out_shape=jax.ShapeDtypeStruct((y_count, z_count, packed, 128), jnp.float32),
        scratch_shapes=[
            pltpu.VMEM((z_count * samples, rows), jnp.bfloat16),
            pltpu.VMEM((256, rows), jnp.bfloat16),
        ],
        compiler_params=pltpu.CompilerParams(vmem_limit_bytes=24 * MIB),
        cost_estimate=pl.CostEstimate(
            flops=2 * y_count * z_count * samples * rows * 256,
            bytes_accessed=3 * MIB,
            transcendentals=0,
        ),
    )(place, owners, adjoint, probes)


def local_call(kernel, out_shape, *args, smem=0, scratch=(), flops=0):
    return pl.pallas_call(
        kernel,
        out_shape=out_shape,
        in_specs=[SMEM] * smem + [VMEM] * (len(args) - smem),
        out_specs=jax.tree.map(lambda _: VMEM, out_shape),
        scratch_shapes=list(scratch),
        compiler_params=pltpu.CompilerParams(vmem_limit_bytes=24 * MIB),
        cost_estimate=pl.CostEstimate(flops=flops, bytes_accessed=2 * MIB, transcendentals=0),
    )(*args)


def merge_kernel(kept_ref, came_ref, own_ref, *out_refs):
    own_ref[...] = kept_ref[0] + came_ref[0]
    for offset, out_ref in enumerate(out_refs, 1):
        out_ref[...] = (kept_ref[offset] + came_ref[offset]).astype(out_ref.dtype)


def gather_kernel(*refs):
    total = refs[0][...]
    for ref in refs[1:-1]:
        total = total + ref[...].astype(jnp.float32)
    refs[-1][...] = total.astype(refs[-1].dtype)


def weights_kernel(place_ref, sums_ref, twiddle_ref, out_ref):
    members, rows, lanes = out_ref.shape
    levels, points = twiddle_ref.shape
    packed = sums_ref.shape[1]
    samples = packed * 2 // 3
    total = jnp.sum(sums_ref[...].astype(jnp.float32), axis=0)
    row = lax.broadcasted_iota(jnp.int32, total.shape, 0)
    lane = lax.broadcasted_iota(jnp.int32, total.shape, 1)
    tail = row - samples + jnp.where(lane < 64, 0, samples // 2)
    sample = place_ref[0] * samples + jnp.where(row < samples, row, tail)
    weights = jnp.where(sample < place_ref[1], total, 0.0).astype(jnp.bfloat16)
    for member in range(members):
        out_ref[member, :packed, :] = weights
        start = pl.multiple_of(member * (points // members) + place_ref[0] * lanes, lanes)
        left = twiddle_ref[:, pl.ds(start, lanes)]
        terms = []
        for _ in range(3):
            term = left.astype(jnp.bfloat16).astype(jnp.float32)
            left = left - term
            terms.append(term)
        terms.append(jnp.zeros((rows - packed - 3 * levels, lanes), jnp.float32))
        out_ref[member, packed:, :] = jnp.concatenate(terms, axis=0).astype(jnp.bfloat16)


def field_kernel(samples_ref, weights_ref, out_ref, field):
    blocks, vectors, points = field.shape
    parts = samples_ref.shape[0] // blocks
    samples = samples_ref.shape[1]
    packed = samples * vectors // 128
    factors = []
    for c in range(blocks):
        head, tail, columns = [], [], []
        for p in range(parts):
            piece = c * parts + p
            head.append(weights_ref[piece, :samples, :])
            rest = weights_ref[piece, samples:packed, :]
            tail += [rest[:, :64], rest[:, 64:]]
            terms = weights_ref[piece, packed:, :].astype(jnp.float32)
            columns.append(terms[0:2] + terms[2:4] + terms[4:6])
        factors.append(jnp.concatenate(columns, axis=1))
        grid = samples_ref[c * parts:(c + 1) * parts].reshape(parts * samples, points)
        head = jnp.concatenate(head, axis=0)
        tail = jnp.concatenate(tail, axis=0)
        field[c, :128, :] = lax.dot_general(
            head, grid, (((0,), (0,)), ((), ())), preferred_element_type=jnp.float32
        )
        field[c, 128:, :] = lax.dot_general(
            tail, grid, (((0,), (0,)), ((), ())), preferred_element_type=jnp.float32
        )
    share = vectors // parts
    for p in range(parts):
        rows = slice(p * share, (p + 1) * share)
        level = [field[c, rows, :] for c in range(blocks)]
        for index, distance in enumerate((2, 1)):
            level = [
                level[c] + factors[c][index:index + 1, :] * level[c ^ distance]
                for c in range(blocks)
            ]
        for c in range(blocks):
            out_ref[c * parts + p] = level[c].astype(jnp.bfloat16)


def turn(x, axis, offset):
    count = lax.axis_size(axis)
    return lax.ppermute(x, axis, [(i, (i + offset) % count) for i in range(count)])


def body(forward_samples, adjoint_samples, probe_values, owners, block_ranks, twiddle):
    groups, parts = lax.axis_size("zg"), lax.axis_size("smp")
    y_count = lax.axis_size("y")
    samples, points = forward_samples.shape
    vectors = probe_values.shape[1]
    members = groups * parts
    piece = points // members
    smp = lax.axis_index("smp")
    y, core = lax.axis_index("y"), lax.axis_index("core")

    pieces = forward_samples.reshape(samples, members, piece).transpose(1, 0, 2)
    own, probes = owners.T, probe_values.T
    pieces, own = lax.optimization_barrier((pieces, own))
    pieces = lax.all_to_all(pieces, GROUP, 0, 0, tiled=True)

    sent = partial_coeffs(jnp.stack([y, 1 - core]), own, adjoint_samples, probes)
    came = lax.ppermute(sent, "core", [(0, 1), (1, 0)])
    kept = partial_coeffs(jnp.stack([y, core]), own, adjoint_samples, probes)
    shape = kept.shape[1:]
    shapes = [jax.ShapeDtypeStruct(shape, jnp.float32)]
    shapes += [jax.ShapeDtypeStruct(shape, jnp.bfloat16)] * (y_count - 1)
    sums = local_call(merge_kernel, shapes, kept, came)
    sums = [sums[0]] + [turn(sums[i], "y", i) for i in range(1, y_count)]
    sums = local_call(gather_kernel, jax.ShapeDtypeStruct(shape, jnp.bfloat16), *sums)
    sums, pieces = lax.optimization_barrier((sums, pieces))
    sums = lax.all_to_all(sums, Z_AXES, 0, 0, tiled=True)
    weights = local_call(
        weights_kernel,
        jax.ShapeDtypeStruct((members, shape[1] + 16, shape[2]), jnp.bfloat16),
        jnp.stack([smp, block_ranks[0]]),
        sums,
        twiddle,
        smem=1,
    )
    weights = lax.all_to_all(weights, GROUP, 0, 0, tiled=True)
    result = local_call(
        field_kernel,
        jax.ShapeDtypeStruct((members, vectors // parts, piece), jnp.bfloat16),
        pieces,
        weights,
        scratch=[pltpu.VMEM((groups, vectors, piece), jnp.float32)],
        flops=2 * members * samples * vectors * piece,
    )
    result = lax.all_to_all(result, GROUP, 0, 0, tiled=True)
    return result.transpose(1, 0, 2).reshape(vectors // parts, points)


def solution(mesh):
    grid = Mesh(mesh.devices.reshape(4, 2, 4, 2, 4), BLK + ("smp",))
    in_specs = (
        P("smp", BLK),
        P("smp", BLK),
        P(BLK, None),
        P(BLK, None),
        P(BLK),
        P(None, BLK),
    )
    out_specs = P("smp", BLK)
    return jax.shard_map(body, mesh=grid, in_specs=in_specs, out_specs=out_specs, check_vma=False)
```

```python
import jax
import jax.numpy as jnp
from jax import lax
from jax.experimental import pallas as pl
from jax.experimental.pallas import tpu as pltpu
from jax.sharding import Mesh, PartitionSpec as P

GROUP = ("zg", "smp")
Z_AXES = ("zg", "zl")
BLK = ("zg", "zl", "y", "core")
MIB = 1024 * 1024
VMEM = pl.BlockSpec(memory_space=pltpu.VMEM)
SMEM = pl.BlockSpec(memory_space=pltpu.SMEM)


def partial_kernel(place_ref, owners_ref, adjoint_ref, probes_ref, out_ref, masked, wide):
    step = pl.program_id(0)
    y_count = pl.num_programs(0)
    z_count = out_ref.shape[1]
    samples = adjoint_ref.shape[0]
    vectors = probes_ref.shape[0]

    @pl.when(step == 0)
    def _():
        wide[:vectors, :] = probes_ref[...]
        wide[vectors:, :] = probes_ref[128:, :]

    own = owners_ref[...]
    adjoint = adjoint_ref[...]
    y = lax.rem(place_ref[0] + step, y_count)
    for offset in range(z_count):
        owner = (offset * y_count + y) * 2 + place_ref[1]
        hot = jnp.where(own == owner, 1.0, 0.0).astype(jnp.bfloat16)
        masked[offset * samples:(offset + 1) * samples, :] = adjoint * hot
    product = lax.dot_general(
        masked[...], wide[...], (((1,), (1,)), ((), ())), preferred_element_type=jnp.float32
    )
    half = samples // 2
    low = lax.broadcasted_iota(jnp.int32, (half, 128), 1) < 64
    for offset in range(z_count):
        block = product[offset * samples:(offset + 1) * samples, :]
        out_ref[0, offset, :samples, :] = block[:, :128]
        out_ref[0, offset, samples:, :] = jnp.where(low, block[:half, 128:], block[half:, 128:])


def partial_coeffs(place, owners, adjoint, probes):
    samples, rows = adjoint.shape
    vectors = probes.shape[0]
    y_count, z_count = lax.axis_size("y"), lax.axis_size(Z_AXES)
    packed = samples * vectors // 128
    return pl.pallas_call(
        partial_kernel,
        grid=(y_count,),
        in_specs=[
            SMEM,
            pl.BlockSpec((1, rows), lambda i: (0, 0)),
            pl.BlockSpec((samples, rows), lambda i: (0, 0)),
            pl.BlockSpec((vectors, rows), lambda i: (0, 0)),
        ],
        out_specs=pl.BlockSpec((1, z_count, packed, 128), lambda i: (i, 0, 0, 0)),
        out_shape=jax.ShapeDtypeStruct((y_count, z_count, packed, 128), jnp.float32),
        scratch_shapes=[
            pltpu.VMEM((z_count * samples, rows), jnp.bfloat16),
            pltpu.VMEM((256, rows), jnp.bfloat16),
        ],
        compiler_params=pltpu.CompilerParams(vmem_limit_bytes=24 * MIB),
        cost_estimate=pl.CostEstimate(
            flops=2 * y_count * z_count * samples * rows * 256,
            bytes_accessed=3 * MIB,
            transcendentals=0,
        ),
    )(place, owners, adjoint, probes)


def local_call(kernel, out_shape, *args, smem=0, scratch=(), flops=0):
    return pl.pallas_call(
        kernel,
        out_shape=out_shape,
        in_specs=[SMEM] * smem + [VMEM] * (len(args) - smem),
        out_specs=jax.tree.map(lambda _: VMEM, out_shape),
        scratch_shapes=list(scratch),
        compiler_params=pltpu.CompilerParams(vmem_limit_bytes=24 * MIB),
        cost_estimate=pl.CostEstimate(flops=flops, bytes_accessed=2 * MIB, transcendentals=0),
    )(*args)


def merge_kernel(kept_ref, came_ref, own_ref, *out_refs):
    own_ref[...] = kept_ref[0] + came_ref[0]
    for offset, out_ref in enumerate(out_refs, 1):
        out_ref[...] = (kept_ref[offset] + came_ref[offset]).astype(out_ref.dtype)


def halve_kernel(place_ref, *refs):
    kept_ref, sent_ref = refs[-2:]
    for block in range(kept_ref.shape[0]):
        for parity, out_ref in ((place_ref[0], kept_ref), (1 - place_ref[0], sent_ref)):
            z = block * 2 + parity
            total = refs[0][z]
            for ref in refs[1:-2]:
                total = total + ref[z].astype(jnp.float32)
            out_ref[block] = total.astype(out_ref.dtype)


def offer_kernel(place_ref, kept_ref, came_ref, twiddle_ref, own_ref, out_ref):
    blocks, packed, lanes = kept_ref.shape
    levels, points = twiddle_ref.shape
    piece = points // (blocks * blocks)
    total = kept_ref[...] + came_ref[...].astype(jnp.float32)
    own_ref[...] = total
    total = total.astype(jnp.bfloat16).reshape(blocks * packed, lanes)
    rank = jnp.full((8 - 3 * levels, lanes), place_ref[1].astype(jnp.float32))
    for block in range(blocks):
        out_ref[block, :blocks * packed, :] = total
        start = (block * blocks + place_ref[0]) * piece
        rows = []
        for column in range(piece // lanes):
            left = twiddle_ref[:, pl.ds(pl.multiple_of(start + column * lanes, lanes), lanes)]
            for _ in range(3):
                term = left.astype(jnp.bfloat16).astype(jnp.float32)
                left = left - term
                rows.append(term)
            rows.append(rank)
        out_ref[block, blocks * packed:, :] = jnp.concatenate(rows, axis=0).astype(jnp.bfloat16)


def weights_kernel(place_ref, own_ref, offers_ref, out_ref):
    blocks, packed, lanes = own_ref.shape
    samples = packed * 2 // 3
    row = lax.broadcasted_iota(jnp.int32, (packed, lanes), 0)
    lane = lax.broadcasted_iota(jnp.int32, (packed, lanes), 1)
    tail = row - samples + jnp.where(lane < 64, 0, samples // 2)
    sample = place_ref[1] * samples + jnp.where(row < samples, row, tail)
    sample = sample.astype(jnp.float32)
    for block in range(blocks):
        total = own_ref[block]
        for other in range(1, blocks):
            partner = place_ref[0] ^ other
            total = total + offers_ref[partner, block * packed:(block + 1) * packed, :].astype(
                jnp.float32
            )
        extra = offers_ref[block, blocks * packed:, :].astype(jnp.float32)
        weights = jnp.where(sample < extra[6:7], total, 0.0).astype(jnp.bfloat16)
        for part in range(out_ref.shape[0]):
            out_ref[part, block] = weights


def field_kernel(samples_ref, offers_ref, weights_ref, out_ref, field):
    blocks, vectors, points = field.shape
    parts = samples_ref.shape[0] // blocks
    samples = samples_ref.shape[1]
    packed = weights_ref.shape[2]
    factors = []
    for c in range(blocks):
        head, tail, columns = [], [], []
        for p in range(parts):
            head.append(weights_ref[p, c, :samples, :])
            rest = weights_ref[p, c, samples:, :]
            tail += [rest[:, :64], rest[:, 64:]]
        extra = offers_ref[c, blocks * packed:, :].astype(jnp.float32)
        for column in range(extra.shape[0] // 8):
            terms = extra[column * 8:column * 8 + 8]
            columns.append(terms[0:2] + terms[2:4] + terms[4:6])
        factors.append(jnp.concatenate(columns, axis=1))
        grid = samples_ref[c * parts:(c + 1) * parts].reshape(parts * samples, points)
        head = jnp.concatenate(head, axis=0)
        tail = jnp.concatenate(tail, axis=0)
        field[c, :128, :] = lax.dot_general(
            head, grid, (((0,), (0,)), ((), ())), preferred_element_type=jnp.float32
        )
        field[c, 128:, :] = lax.dot_general(
            tail, grid, (((0,), (0,)), ((), ())), preferred_element_type=jnp.float32
        )
    share = vectors // parts
    for p in range(parts):
        rows = slice(p * share, (p + 1) * share)
        level = [field[c, rows, :] for c in range(blocks)]
        for index, distance in enumerate((2, 1)):
            level = [
                level[c] + factors[c][index:index + 1, :] * level[c ^ distance]
                for c in range(blocks)
            ]
        for c in range(blocks):
            out_ref[c * parts + p] = level[c].astype(jnp.bfloat16)


def turn(x, axis, offset):
    count = lax.axis_size(axis)
    return lax.ppermute(x, axis, [(i, (i + offset) % count) for i in range(count)])


def body(forward_samples, adjoint_samples, probe_values, owners, block_ranks, twiddle):
    groups, parts = lax.axis_size("zg"), lax.axis_size("smp")
    y_count = lax.axis_size("y")
    samples, points = forward_samples.shape
    vectors = probe_values.shape[1]
    members = groups * parts
    piece = points // members
    smp = lax.axis_index("smp")
    y, core = lax.axis_index("y"), lax.axis_index("core")

    pieces = forward_samples.reshape(samples, members, piece).transpose(1, 0, 2)
    own, probes = owners.T, probe_values.T
    pieces, own = lax.optimization_barrier((pieces, own))
    pieces = lax.all_to_all(pieces, GROUP, 0, 0, tiled=True)

    sent = partial_coeffs(jnp.stack([y, 1 - core]), own, adjoint_samples, probes)
    came = lax.ppermute(sent, "core", [(0, 1), (1, 0)])
    kept = partial_coeffs(jnp.stack([y, core]), own, adjoint_samples, probes)
    shape = kept.shape[1:]
    shapes = [jax.ShapeDtypeStruct(shape, jnp.float32)]
    shapes += [jax.ShapeDtypeStruct(shape, jnp.bfloat16)] * (y_count - 1)
    sums = local_call(merge_kernel, shapes, kept, came)
    sums = [sums[0]] + [turn(sums[i], "y", i) for i in range(1, y_count)]
    shape = (groups,) + shape[1:]
    shapes = [jax.ShapeDtypeStruct(shape, jnp.float32), jax.ShapeDtypeStruct(shape, jnp.bfloat16)]
    zl = lax.axis_index("zl")
    kept, sent = local_call(halve_kernel, shapes, zl[None], *sums, smem=1)
    came = lax.ppermute(sent, "zl", [(0, 1), (1, 0)])
    rows = groups * shape[1] + 8 * piece // shape[2]
    shapes = [jax.ShapeDtypeStruct(shape, jnp.float32)]
    shapes += [jax.ShapeDtypeStruct((groups, rows, shape[2]), jnp.bfloat16)]
    place = jnp.stack([smp, block_ranks[0]])
    partial, offers = local_call(offer_kernel, shapes, place, kept, came, twiddle, smem=1)
    offers, pieces = lax.optimization_barrier((offers, pieces))
    offers = lax.all_to_all(offers, "zg", 0, 0, tiled=True)
    weights = local_call(
        weights_kernel,
        jax.ShapeDtypeStruct((parts,) + shape, jnp.bfloat16),
        jnp.stack([lax.axis_index("zg"), smp]),
        partial,
        offers,
        smem=1,
    )
    weights = lax.all_to_all(weights, "smp", 0, 0, tiled=True)
    result = local_call(
        field_kernel,
        jax.ShapeDtypeStruct((members, vectors // parts, piece), jnp.bfloat16),
        pieces,
        offers,
        weights,
        scratch=[pltpu.VMEM((groups, vectors, piece), jnp.float32)],
        flops=2 * members * samples * vectors * piece,
    )
    result = lax.all_to_all(result, GROUP, 0, 0, tiled=True)
    return result.transpose(1, 0, 2).reshape(vectors // parts, points)


def solution(mesh):
    grid = Mesh(mesh.devices.reshape(4, 2, 4, 2, 4), BLK + ("smp",))
    in_specs = (
        P("smp", BLK),
        P("smp", BLK),
        P(BLK, None),
        P(BLK, None),
        P(BLK),
        P(None, BLK),
    )
    out_specs = P("smp", BLK)
    return jax.shard_map(body, mesh=grid, in_specs=in_specs, out_specs=out_specs, check_vma=False)
```

```python
import jax
import jax.numpy as jnp
from jax import lax
from jax.experimental import pallas as pl
from jax.experimental.pallas import tpu as pltpu
from jax.sharding import Mesh, PartitionSpec as P

GROUP = ("zg", "smp")
Z_AXES = ("zg", "zl")
BLK = ("zg", "zl", "y", "core")
MIB = 1024 * 1024
VMEM = pl.BlockSpec(memory_space=pltpu.VMEM)
SMEM = pl.BlockSpec(memory_space=pltpu.SMEM)


def partial_kernel(place_ref, owners_ref, adjoint_ref, probes_ref, out_ref, masked, wide):
    step = pl.program_id(0)
    y_count = pl.num_programs(0)
    z_count = out_ref.shape[1]
    samples = adjoint_ref.shape[0]
    vectors = probes_ref.shape[0]

    @pl.when(step == 0)
    def _():
        wide[:vectors, :] = probes_ref[...]
        wide[vectors:, :] = probes_ref[128:, :]

    own = owners_ref[...]
    adjoint = adjoint_ref[...]
    y = lax.rem(place_ref[0] + step, y_count)
    for offset in range(z_count):
        owner = (offset * y_count + y) * 2 + place_ref[1]
        hot = jnp.where(own == owner, 1.0, 0.0).astype(jnp.bfloat16)
        masked[offset * samples:(offset + 1) * samples, :] = adjoint * hot
    product = lax.dot_general(
        masked[...], wide[...], (((1,), (1,)), ((), ())), preferred_element_type=jnp.float32
    )
    half = samples // 2
    low = lax.broadcasted_iota(jnp.int32, (half, 128), 1) < 64
    for offset in range(z_count):
        block = product[offset * samples:(offset + 1) * samples, :]
        out_ref[0, offset, :samples, :] = block[:, :128]
        out_ref[0, offset, samples:, :] = jnp.where(low, block[:half, 128:], block[half:, 128:])


def partial_coeffs(place, owners, adjoint, probes):
    samples, rows = adjoint.shape
    vectors = probes.shape[0]
    y_count, z_count = lax.axis_size("y"), lax.axis_size(Z_AXES)
    packed = samples * vectors // 128
    return pl.pallas_call(
        partial_kernel,
        grid=(y_count,),
        in_specs=[
            SMEM,
            pl.BlockSpec((1, rows), lambda i: (0, 0)),
            pl.BlockSpec((samples, rows), lambda i: (0, 0)),
            pl.BlockSpec((vectors, rows), lambda i: (0, 0)),
        ],
        out_specs=pl.BlockSpec((1, z_count, packed, 128), lambda i: (i, 0, 0, 0)),
        out_shape=jax.ShapeDtypeStruct((y_count, z_count, packed, 128), jnp.float32),
        scratch_shapes=[
            pltpu.VMEM((z_count * samples, rows), jnp.bfloat16),
            pltpu.VMEM((256, rows), jnp.bfloat16),
        ],
        compiler_params=pltpu.CompilerParams(vmem_limit_bytes=24 * MIB),
        cost_estimate=pl.CostEstimate(
            flops=2 * y_count * z_count * samples * rows * 256,
            bytes_accessed=3 * MIB,
            transcendentals=0,
        ),
    )(place, owners, adjoint, probes)


def local_call(kernel, out_shape, *args, smem=0, scratch=(), flops=0):
    return pl.pallas_call(
        kernel,
        out_shape=out_shape,
        in_specs=[SMEM] * smem + [VMEM] * (len(args) - smem),
        out_specs=jax.tree.map(lambda _: VMEM, out_shape),
        scratch_shapes=list(scratch),
        compiler_params=pltpu.CompilerParams(vmem_limit_bytes=24 * MIB),
        cost_estimate=pl.CostEstimate(flops=flops, bytes_accessed=2 * MIB, transcendentals=0),
    )(*args)


def merge_kernel(kept_ref, came_ref, own_ref, *out_refs):
    own_ref[...] = kept_ref[0] + came_ref[0]
    for offset, out_ref in enumerate(out_refs, 1):
        out_ref[...] = (kept_ref[offset] + came_ref[offset]).astype(out_ref.dtype)


def halve_kernel(place_ref, *refs):
    kept_ref, sent_ref = refs[-2:]
    for block in range(kept_ref.shape[0]):
        for parity, out_ref in ((place_ref[0], kept_ref), (1 - place_ref[0], sent_ref)):
            z = block * 2 + parity
            total = refs[0][z]
            for ref in refs[1:-2]:
                total = total + ref[z].astype(jnp.float32)
            out_ref[block] = total.astype(out_ref.dtype)


def offer_kernel(place_ref, kept_ref, came_ref, twiddle_ref, own_ref, extra_ref, *refs):
    out_refs, total = refs[:-1], refs[-1]
    zg, smp, rank = place_ref[0], place_ref[1], place_ref[2]
    blocks, packed, lanes = kept_ref.shape
    levels, points = twiddle_ref.shape
    piece = points // (blocks * blocks)
    total[...] = kept_ref[...] + came_ref[...].astype(jnp.float32)
    rank = jnp.full((8 - 3 * levels, lanes), rank.astype(jnp.float32))
    for distance in range(blocks):
        partner = zg ^ distance
        start = (partner * blocks + smp) * piece
        rows = []
        for column in range(piece // lanes):
            left = twiddle_ref[:, pl.ds(pl.multiple_of(start + column * lanes, lanes), lanes)]
            for _ in range(3):
                term = left.astype(jnp.bfloat16).astype(jnp.float32)
                left = left - term
                rows.append(term)
            rows.append(rank)
        rows = jnp.concatenate(rows, axis=0).astype(jnp.bfloat16)
        for block in range(blocks):
            value = total[partner ^ block]
            if distance == 0:
                own_ref[block] = value
            else:
                target = slice(block * packed, (block + 1) * packed)
                out_refs[distance - 1][target, :] = value.astype(jnp.bfloat16)
        if distance == 0:
            extra_ref[...] = rows
        else:
            out_refs[distance - 1][blocks * packed:, :] = rows


def weights_kernel(place_ref, own_ref, extra_ref, *refs):
    offers, out_ref = refs[:-1], refs[-1]
    blocks, packed, lanes = own_ref.shape
    samples = packed * 2 // 3
    row = lax.broadcasted_iota(jnp.int32, (packed, lanes), 0)
    lane = lax.broadcasted_iota(jnp.int32, (packed, lanes), 1)
    tail = row - samples + jnp.where(lane < 64, 0, samples // 2)
    sample = place_ref[1] * samples + jnp.where(row < samples, row, tail)
    sample = sample.astype(jnp.float32)
    for block in range(blocks):
        total = own_ref[block]
        for offer in offers:
            total = total + offer[block * packed:(block + 1) * packed, :].astype(jnp.float32)
        extra = offers[block - 1][blocks * packed:, :] if block else extra_ref[...]
        rank = extra.astype(jnp.float32)[6:7]
        out_ref[block] = jnp.where(sample < rank, total, 0.0).astype(jnp.bfloat16)


def field_kernel(blocks, parts, place_ref, samples_ref, extra_ref, *refs):
    offers, weight_refs = refs[:blocks - 1], refs[blocks - 1:-2]
    out_ref, field = refs[-2:]
    zg, smp = place_ref[0], place_ref[1]
    vectors, points = field.shape[1:]
    samples = samples_ref.shape[1]
    packed = weight_refs[0].shape[1]
    factors = []
    for c in range(blocks):
        head, tail, columns, grid = [], [], [], []
        for p in range(parts):
            grid.append(samples_ref[(zg ^ c) * parts + lax.rem(smp - p + parts, parts)])
            head.append(weight_refs[p][c, :samples, :])
            rest = weight_refs[p][c, samples:, :]
            tail += [rest[:, :64], rest[:, 64:]]
        extra = offers[c - 1][blocks * packed:, :] if c else extra_ref[...]
        extra = extra.astype(jnp.float32)
        for column in range(extra.shape[0] // 8):
            terms = extra[column * 8:column * 8 + 8]
            columns.append(terms[0:2] + terms[2:4] + terms[4:6])
        factors.append(jnp.concatenate(columns, axis=1))
        grid = jnp.concatenate(grid, axis=0)
        head = jnp.concatenate(head, axis=0)
        tail = jnp.concatenate(tail, axis=0)
        field[c, :128, :] = lax.dot_general(
            head, grid, (((0,), (0,)), ((), ())), preferred_element_type=jnp.float32
        )
        field[c, 128:, :] = lax.dot_general(
            tail, grid, (((0,), (0,)), ((), ())), preferred_element_type=jnp.float32
        )
    share = vectors // parts
    for p in range(parts):
        rows = slice(p * share, (p + 1) * share)
        level = [field[c, rows, :] for c in range(blocks)]
        for index, distance in enumerate((2, 1)):
            level = [
                level[c] + factors[c][index:index + 1, :] * level[c ^ distance]
                for c in range(blocks)
            ]
        for c in range(blocks):
            out_ref[(zg ^ c) * parts + p] = level[c].astype(jnp.bfloat16)


def exchange(pieces, axis, route):
    count = lax.axis_size(axis)
    came = {}
    for offset in sorted(pieces, key=lambda k: abs(k - count // 2)):
        pairs = [(i, route(i, offset) % count) for i in range(count)]
        came[offset] = lax.ppermute(pieces[offset], axis, pairs)
    return [came[offset] for offset in sorted(pieces)]


def body(forward_samples, adjoint_samples, probe_values, owners, block_ranks, twiddle):
    groups, parts = lax.axis_size("zg"), lax.axis_size("smp")
    y_count = lax.axis_size("y")
    samples, points = forward_samples.shape
    vectors = probe_values.shape[1]
    members = groups * parts
    piece = points // members
    smp = lax.axis_index("smp")
    y, core = lax.axis_index("y"), lax.axis_index("core")

    pieces = forward_samples.reshape(samples, members, piece).transpose(1, 0, 2)
    own, probes = owners.T, probe_values.T
    pieces, own = lax.optimization_barrier((pieces, own))
    pieces = lax.all_to_all(pieces, GROUP, 0, 0, tiled=True)

    sent = partial_coeffs(jnp.stack([y, 1 - core]), own, adjoint_samples, probes)
    came = lax.ppermute(sent, "core", [(0, 1), (1, 0)])
    kept = partial_coeffs(jnp.stack([y, core]), own, adjoint_samples, probes)
    shape = kept.shape[1:]
    shapes = [jax.ShapeDtypeStruct(shape, jnp.float32)]
    shapes += [jax.ShapeDtypeStruct(shape, jnp.bfloat16)] * (y_count - 1)
    sums = local_call(merge_kernel, shapes, kept, came)
    came = exchange(dict(enumerate(sums[1:], 1)), "y", lambda i, k: i + k)
    sums = [sums[0]] + came
    shape = (groups,) + shape[1:]
    shapes = [jax.ShapeDtypeStruct(shape, jnp.float32), jax.ShapeDtypeStruct(shape, jnp.bfloat16)]
    zl = lax.axis_index("zl")
    kept, sent = local_call(halve_kernel, shapes, zl[None], *sums, smem=1)
    came = lax.ppermute(sent, "zl", [(0, 1), (1, 0)])
    tail = 8 * piece // shape[2]
    shapes = [jax.ShapeDtypeStruct(shape, jnp.float32)]
    shapes += [jax.ShapeDtypeStruct((tail, shape[2]), jnp.bfloat16)]
    offer = (groups * shape[1] + tail, shape[2])
    shapes += [jax.ShapeDtypeStruct(offer, jnp.bfloat16)] * (groups - 1)
    zg = lax.axis_index("zg")
    place = jnp.stack([zg, smp, block_ranks[0]])
    partial, extra, *offers = local_call(
        offer_kernel,
        shapes,
        place,
        kept,
        came,
        twiddle,
        smem=1,
        scratch=[pltpu.VMEM(shape, jnp.float32)],
    )
    offers = exchange(dict(enumerate(offers, 1)), "zg", lambda i, k: i ^ k)
    weights = local_call(
        weights_kernel,
        jax.ShapeDtypeStruct(shape, jnp.bfloat16),
        place,
        partial,
        extra,
        *offers,
        smem=1,
    )
    others = exchange({p: weights for p in range(1, parts)}, "smp", lambda i, k: i + k)
    result = local_call(
        lambda *refs: field_kernel(groups, parts, *refs),
        jax.ShapeDtypeStruct((members, vectors // parts, piece), jnp.bfloat16),
        place,
        pieces,
        extra,
        *offers,
        weights,
        *others,
        smem=1,
        scratch=[pltpu.VMEM((groups, vectors, piece), jnp.float32)],
        flops=2 * members * samples * vectors * piece,
    )
    result = lax.all_to_all(result, GROUP, 0, 0, tiled=True)
    return result.transpose(1, 0, 2).reshape(vectors // parts, points)


def solution(mesh):
    grid = Mesh(mesh.devices.reshape(4, 2, 4, 2, 4), BLK + ("smp",))
    in_specs = (
        P("smp", BLK),
        P("smp", BLK),
        P(BLK, None),
        P(BLK, None),
        P(BLK),
        P(None, BLK),
    )
    out_specs = P("smp", BLK)
    return jax.shard_map(body, mesh=grid, in_specs=in_specs, out_specs=out_specs, check_vma=False)
```

```python
import jax
import jax.numpy as jnp
from jax import lax
from jax.experimental import pallas as pl
from jax.experimental.pallas import tpu as pltpu
from jax.sharding import Mesh, PartitionSpec as P

GROUP = ("zg", "smp")
Z_AXES = ("zg", "zl")
BLK = ("zg", "zl", "y", "core")
MIB = 1024 * 1024
VMEM = pl.BlockSpec(memory_space=pltpu.VMEM)
SMEM = pl.BlockSpec(memory_space=pltpu.SMEM)


def partial_kernel(place_ref, owners_ref, adjoint_ref, probes_ref, out_ref, masked, wide):
    step = pl.program_id(0)
    y_count = pl.num_programs(0)
    z_count = out_ref.shape[1]
    samples = adjoint_ref.shape[0]
    vectors = probes_ref.shape[0]

    @pl.when(step == 0)
    def _():
        wide[:vectors, :] = probes_ref[...]
        wide[vectors:, :] = probes_ref[128:, :]

    own = owners_ref[...]
    adjoint = adjoint_ref[...]
    y = lax.rem(place_ref[0] + step, y_count)
    for offset in range(z_count):
        owner = (offset * y_count + y) * 2 + place_ref[1]
        hot = jnp.where(own == owner, 1.0, 0.0).astype(jnp.bfloat16)
        masked[offset * samples:(offset + 1) * samples, :] = adjoint * hot
    product = lax.dot_general(
        masked[...], wide[...], (((1,), (1,)), ((), ())), preferred_element_type=jnp.float32
    )
    half = samples // 2
    low = lax.broadcasted_iota(jnp.int32, (half, 128), 1) < 64
    for offset in range(z_count):
        block = product[offset * samples:(offset + 1) * samples, :]
        out_ref[0, offset, :samples, :] = block[:, :128]
        out_ref[0, offset, samples:, :] = jnp.where(low, block[:half, 128:], block[half:, 128:])


def partial_coeffs(place, owners, adjoint, probes):
    samples, rows = adjoint.shape
    vectors = probes.shape[0]
    y_count, z_count = lax.axis_size("y"), lax.axis_size(Z_AXES)
    packed = samples * vectors // 128
    return pl.pallas_call(
        partial_kernel,
        grid=(y_count,),
        in_specs=[
            SMEM,
            pl.BlockSpec((1, rows), lambda i: (0, 0)),
            pl.BlockSpec((samples, rows), lambda i: (0, 0)),
            pl.BlockSpec((vectors, rows), lambda i: (0, 0)),
        ],
        out_specs=pl.BlockSpec((1, z_count, packed, 128), lambda i: (i, 0, 0, 0)),
        out_shape=jax.ShapeDtypeStruct((y_count, z_count, packed, 128), jnp.float32),
        scratch_shapes=[
            pltpu.VMEM((z_count * samples, rows), jnp.bfloat16),
            pltpu.VMEM((256, rows), jnp.bfloat16),
        ],
        compiler_params=pltpu.CompilerParams(vmem_limit_bytes=24 * MIB),
        cost_estimate=pl.CostEstimate(
            flops=2 * y_count * z_count * samples * rows * 256,
            bytes_accessed=3 * MIB,
            transcendentals=0,
        ),
    )(place, owners, adjoint, probes)


def local_call(kernel, out_shape, *args, smem=0, scratch=(), flops=0):
    return pl.pallas_call(
        kernel,
        out_shape=out_shape,
        in_specs=[SMEM] * smem + [VMEM] * (len(args) - smem),
        out_specs=jax.tree.map(lambda _: VMEM, out_shape),
        scratch_shapes=list(scratch),
        compiler_params=pltpu.CompilerParams(vmem_limit_bytes=24 * MIB),
        cost_estimate=pl.CostEstimate(flops=flops, bytes_accessed=2 * MIB, transcendentals=0),
    )(*args)


def merge_kernel(kept_ref, came_ref, own_ref, *out_refs):
    own_ref[...] = kept_ref[0] + came_ref[0]
    for offset, out_ref in enumerate(out_refs, 1):
        out_ref[...] = (kept_ref[offset] + came_ref[offset]).astype(out_ref.dtype)


def halve_kernel(place_ref, *refs):
    kept_ref, sent_ref = refs[-2:]
    for block in range(kept_ref.shape[0]):
        for parity, out_ref in ((place_ref[0], kept_ref), (1 - place_ref[0], sent_ref)):
            z = block * 2 + parity
            total = refs[0][z]
            for ref in refs[1:-2]:
                total = total + ref[z].astype(jnp.float32)
            out_ref[block] = total.astype(out_ref.dtype)


def offer_kernel(place_ref, kept_ref, came_ref, twiddle_ref, own_ref, extra_ref, *refs):
    out_refs, total = refs[:-1], refs[-1]
    zg, smp, rank = place_ref[0], place_ref[1], place_ref[2]
    blocks, packed, lanes = kept_ref.shape
    levels, points = twiddle_ref.shape
    piece = points // (blocks * blocks)
    total[...] = kept_ref[...] + came_ref[...].astype(jnp.float32)
    rank = jnp.full((8 - 3 * levels, lanes), rank.astype(jnp.float32))
    for distance in range(blocks):
        partner = zg ^ distance
        start = (partner * blocks + smp) * piece
        rows = []
        for column in range(piece // lanes):
            left = twiddle_ref[:, pl.ds(pl.multiple_of(start + column * lanes, lanes), lanes)]
            for _ in range(3):
                term = left.astype(jnp.bfloat16).astype(jnp.float32)
                left = left - term
                rows.append(term)
            rows.append(rank)
        rows = jnp.concatenate(rows, axis=0).astype(jnp.bfloat16)
        for block in range(blocks):
            value = total[partner ^ block]
            if distance == 0:
                own_ref[block] = value
            else:
                target = slice(block * packed, (block + 1) * packed)
                out_refs[distance - 1][target, :] = value.astype(jnp.bfloat16)
        if distance == 0:
            extra_ref[...] = rows
        else:
            out_refs[distance - 1][blocks * packed:, :] = rows


def weights_kernel(place_ref, own_ref, extra_ref, *refs):
    offers, out_ref = refs[:-1], refs[-1]
    blocks, packed, lanes = own_ref.shape
    samples = packed * 2 // 3
    row = lax.broadcasted_iota(jnp.int32, (packed, lanes), 0)
    lane = lax.broadcasted_iota(jnp.int32, (packed, lanes), 1)
    tail = row - samples + jnp.where(lane < 64, 0, samples // 2)
    sample = place_ref[1] * samples + jnp.where(row < samples, row, tail)
    sample = sample.astype(jnp.float32)
    for block in range(blocks):
        total = own_ref[block]
        for offer in offers:
            total = total + offer[block * packed:(block + 1) * packed, :].astype(jnp.float32)
        extra = offers[block - 1][blocks * packed:, :] if block else extra_ref[...]
        rank = extra.astype(jnp.float32)[6:7]
        out_ref[block] = jnp.where(sample < rank, total, 0.0).astype(jnp.bfloat16)


def field_kernel(blocks, parts, place_ref, samples_ref, extra_ref, *refs):
    offers, weight_refs = refs[:blocks - 1], refs[blocks - 1:-2]
    out_ref, field = refs[-2:]
    zg, smp = place_ref[0], place_ref[1]
    vectors, points = field.shape[1:]
    samples = samples_ref.shape[1]
    packed = weight_refs[0].shape[1]
    factors = []
    for c in range(blocks):
        head, tail, columns, grid = [], [], [], []
        for p in range(parts):
            grid.append(samples_ref[(zg ^ c) * parts + lax.rem(smp - p + parts, parts)])
            head.append(weight_refs[p][c, :samples, :])
            rest = weight_refs[p][c, samples:, :]
            tail += [rest[:, :64], rest[:, 64:]]
        extra = offers[c - 1][blocks * packed:, :] if c else extra_ref[...]
        extra = extra.astype(jnp.float32)
        for column in range(extra.shape[0] // 8):
            terms = extra[column * 8:column * 8 + 8]
            columns.append(terms[0:2] + terms[2:4] + terms[4:6])
        factors.append(jnp.concatenate(columns, axis=1))
        grid = jnp.concatenate(grid, axis=0)
        head = jnp.concatenate(head, axis=0)
        tail = jnp.concatenate(tail, axis=0)
        field[c, :128, :] = lax.dot_general(
            head, grid, (((0,), (0,)), ((), ())), preferred_element_type=jnp.float32
        )
        field[c, 128:, :] = lax.dot_general(
            tail, grid, (((0,), (0,)), ((), ())), preferred_element_type=jnp.float32
        )
    share = vectors // parts
    for p in range(parts):
        rows = slice(p * share, (p + 1) * share)
        level = [field[c, rows, :] for c in range(blocks)]
        for index, distance in enumerate((2, 1)):
            level = [
                level[c] + factors[c][index:index + 1, :] * level[c ^ distance]
                for c in range(blocks)
            ]
        for c in range(blocks):
            out_ref[(zg ^ c) * parts + p] = level[c].astype(jnp.bfloat16)


def exchange(pieces, axis, route):
    count = lax.axis_size(axis)
    came = {}
    for offset in sorted(pieces, key=lambda k: abs(k - count // 2)):
        pairs = [(i, route(i, offset) % count) for i in range(count)]
        came[offset] = lax.ppermute(pieces[offset], axis, pairs)
    return [came[offset] for offset in sorted(pieces)]


def body(forward_samples, adjoint_samples, probe_values, owners, block_ranks, twiddle):
    groups, parts = lax.axis_size("zg"), lax.axis_size("smp")
    y_count = lax.axis_size("y")
    samples, points = forward_samples.shape
    vectors = probe_values.shape[1]
    members = groups * parts
    piece = points // members
    smp = lax.axis_index("smp")
    y, core = lax.axis_index("y"), lax.axis_index("core")

    pieces = forward_samples.reshape(samples, members, piece).transpose(1, 0, 2)
    own, probes = owners.T, probe_values.T
    pieces, own = lax.optimization_barrier((pieces, own))
    pieces = lax.all_to_all(pieces, GROUP, 0, 0, tiled=True)

    sent = partial_coeffs(jnp.stack([y, 1 - core]), own, adjoint_samples, probes)
    came = lax.ppermute(sent, "core", [(0, 1), (1, 0)])
    kept = partial_coeffs(jnp.stack([y, core]), own, adjoint_samples, probes)
    shape = kept.shape[1:]
    shapes = [jax.ShapeDtypeStruct(shape, jnp.float32)]
    shapes += [jax.ShapeDtypeStruct(shape, jnp.bfloat16)] * (y_count - 1)
    sums = local_call(merge_kernel, shapes, kept, came)
    came = exchange(dict(enumerate(sums[1:], 1)), "y", lambda i, k: i + k)
    sums = [sums[0]] + came
    shape = (groups,) + shape[1:]
    shapes = [jax.ShapeDtypeStruct(shape, jnp.float32), jax.ShapeDtypeStruct(shape, jnp.bfloat16)]
    zl = lax.axis_index("zl")
    kept, sent = local_call(halve_kernel, shapes, zl[None], *sums, smem=1)
    came = lax.ppermute(sent, "zl", [(0, 1), (1, 0)])
    tail = 8 * piece // shape[2]
    shapes = [jax.ShapeDtypeStruct(shape, jnp.float32)]
    shapes += [jax.ShapeDtypeStruct((tail, shape[2]), jnp.bfloat16)]
    offer = (groups * shape[1] + tail, shape[2])
    shapes += [jax.ShapeDtypeStruct(offer, jnp.bfloat16)] * (groups - 1)
    zg = lax.axis_index("zg")
    place = jnp.stack([zg, smp, block_ranks[0]])
    partial, extra, *offers = local_call(
        offer_kernel,
        shapes,
        place,
        kept,
        came,
        twiddle,
        smem=1,
        scratch=[pltpu.VMEM(shape, jnp.float32)],
    )
    *offers, pieces = lax.optimization_barrier((*offers, pieces))
    offers = exchange(dict(enumerate(offers, 1)), "zg", lambda i, k: i ^ k)
    weights = local_call(
        weights_kernel,
        jax.ShapeDtypeStruct(shape, jnp.bfloat16),
        place,
        partial,
        extra,
        *offers,
        smem=1,
    )
    others = exchange({p: weights for p in range(1, parts)}, "smp", lambda i, k: i + k)
    result = local_call(
        lambda *refs: field_kernel(groups, parts, *refs),
        jax.ShapeDtypeStruct((members, vectors // parts, piece), jnp.bfloat16),
        place,
        pieces,
        extra,
        *offers,
        weights,
        *others,
        smem=1,
        scratch=[pltpu.VMEM((groups, vectors, piece), jnp.float32)],
        flops=2 * members * samples * vectors * piece,
    )
    result = lax.all_to_all(result, GROUP, 0, 0, tiled=True)
    return result.transpose(1, 0, 2).reshape(vectors // parts, points)


def solution(mesh):
    grid = Mesh(mesh.devices.reshape(4, 2, 4, 2, 4), BLK + ("smp",))
    in_specs = (
        P("smp", BLK),
        P("smp", BLK),
        P(BLK, None),
        P(BLK, None),
        P(BLK),
        P(None, BLK),
    )
    out_specs = P("smp", BLK)
    return jax.shard_map(body, mesh=grid, in_specs=in_specs, out_specs=out_specs, check_vma=False)
```

```python
import jax
import jax.numpy as jnp
from jax import lax
from jax.experimental import pallas as pl
from jax.experimental.pallas import tpu as pltpu
from jax.sharding import Mesh, PartitionSpec as P

GROUP = ("zg", "smp")
Z_AXES = ("zg", "zl")
BLK = ("zg", "zl", "y", "core")
MIB = 1024 * 1024
VMEM = pl.BlockSpec(memory_space=pltpu.VMEM)
SMEM = pl.BlockSpec(memory_space=pltpu.SMEM)


def split_kernel(source_ref, out_ref, sems):
    pieces, _, points = out_ref.shape
    copies = [
        pltpu.make_async_copy(source_ref.at[:, pl.ds(i * points, points)], out_ref.at[i], sems.at[i])
        for i in range(pieces)
    ]
    for copy in copies:
        copy.start()
    for copy in copies:
        copy.wait()


def split(source, pieces):
    rows, points = source.shape
    return pl.pallas_call(
        split_kernel,
        out_shape=jax.ShapeDtypeStruct((pieces, rows, points // pieces), source.dtype),
        in_specs=[pl.BlockSpec(memory_space=pl.ANY)],
        out_specs=VMEM,
        scratch_shapes=[pltpu.SemaphoreType.DMA((pieces,))],
        compiler_params=pltpu.CompilerParams(vmem_limit_bytes=56 * MIB),
        cost_estimate=pl.CostEstimate(flops=0, bytes_accessed=2 * MIB, transcendentals=0),
    )(source)


def partial_kernel(y_count, offset, other, place_ref, owners_ref, adjoint_ref, wide_ref, *refs):
    out_ref, masked = refs[-2:]
    samples = adjoint_ref.shape[0]
    z_count = out_ref.shape[0]
    own = owners_ref[...]
    adjoint = adjoint_ref[...]
    y = lax.rem(place_ref[0] + offset, y_count)
    core = 1 - place_ref[1] if other else place_ref[1]
    for z in range(z_count):
        hot = jnp.where(own == (z * y_count + y) * 2 + core, 1.0, 0.0).astype(jnp.bfloat16)
        masked[z * samples:(z + 1) * samples, :] = adjoint * hot
    product = lax.dot_general(
        masked[...], wide_ref[...], (((1,), (1,)), ((), ())), preferred_element_type=jnp.float32
    )
    half = samples // 2
    low = lax.broadcasted_iota(jnp.int32, (half, 128), 1) < 64
    for z in range(z_count):
        block = product[z * samples:(z + 1) * samples, :]
        head = block[:, :128]
        tail = jnp.where(low, block[:half, 128:], block[half:, 128:])
        if not other:
            head = head + refs[0][z, :samples, :]
            tail = tail + refs[0][z, samples:, :]
        out_ref[z, :samples, :] = head.astype(out_ref.dtype)
        out_ref[z, samples:, :] = tail.astype(out_ref.dtype)


def local_call(kernel, out_shape, *args, smem=0, scratch=(), flops=0):
    return pl.pallas_call(
        kernel,
        out_shape=out_shape,
        in_specs=[SMEM] * smem + [VMEM] * (len(args) - smem),
        out_specs=jax.tree.map(lambda _: VMEM, out_shape),
        scratch_shapes=list(scratch),
        compiler_params=pltpu.CompilerParams(vmem_limit_bytes=24 * MIB),
        cost_estimate=pl.CostEstimate(flops=flops, bytes_accessed=2 * MIB, transcendentals=0),
    )(*args)


def halve_kernel(place_ref, *refs):
    kept_ref, sent_ref = refs[-2:]
    for block in range(kept_ref.shape[0]):
        for parity, out_ref in ((place_ref[0], kept_ref), (1 - place_ref[0], sent_ref)):
            z = block * 2 + parity
            total = refs[0][z]
            for ref in refs[1:-2]:
                total = total + ref[z].astype(jnp.float32)
            out_ref[block] = total.astype(out_ref.dtype)


def offer_kernel(place_ref, kept_ref, came_ref, twiddle_ref, own_ref, extra_ref, *refs):
    out_refs, total = refs[:-1], refs[-1]
    zg, smp, rank = place_ref[0], place_ref[1], place_ref[2]
    blocks, packed, lanes = kept_ref.shape
    levels, points = twiddle_ref.shape
    piece = points // (blocks * blocks)
    total[...] = kept_ref[...] + came_ref[...].astype(jnp.float32)
    rank = jnp.full((8 - 3 * levels, lanes), rank.astype(jnp.float32))
    for distance in range(blocks):
        partner = zg ^ distance
        start = (partner * blocks + smp) * piece
        rows = []
        for column in range(piece // lanes):
            left = twiddle_ref[:, pl.ds(pl.multiple_of(start + column * lanes, lanes), lanes)]
            for _ in range(3):
                term = left.astype(jnp.bfloat16).astype(jnp.float32)
                left = left - term
                rows.append(term)
            rows.append(rank)
        rows = jnp.concatenate(rows, axis=0).astype(jnp.bfloat16)
        for block in range(blocks):
            value = total[partner ^ block]
            if distance == 0:
                own_ref[block] = value
            else:
                target = slice(block * packed, (block + 1) * packed)
                out_refs[distance - 1][target, :] = value.astype(jnp.bfloat16)
        if distance == 0:
            extra_ref[...] = rows
        else:
            out_refs[distance - 1][blocks * packed:, :] = rows


def weights_kernel(place_ref, own_ref, extra_ref, *refs):
    offers, out_ref = refs[:-1], refs[-1]
    blocks, packed, lanes = own_ref.shape
    samples = packed * 2 // 3
    row = lax.broadcasted_iota(jnp.int32, (packed, lanes), 0)
    lane = lax.broadcasted_iota(jnp.int32, (packed, lanes), 1)
    tail = row - samples + jnp.where(lane < 64, 0, samples // 2)
    sample = place_ref[1] * samples + jnp.where(row < samples, row, tail)
    sample = sample.astype(jnp.float32)
    for block in range(blocks):
        total = own_ref[block]
        for offer in offers:
            total = total + offer[block * packed:(block + 1) * packed, :].astype(jnp.float32)
        extra = offers[block - 1][blocks * packed:, :] if block else extra_ref[...]
        rank = extra.astype(jnp.float32)[6:7]
        out_ref[block] = jnp.where(sample < rank, total, 0.0).astype(jnp.bfloat16)


def field_kernel(blocks, parts, place_ref, samples_ref, extra_ref, *refs):
    offers, weight_refs = refs[:blocks - 1], refs[blocks - 1:-2]
    out_ref, field = refs[-2:]
    zg, smp = place_ref[0], place_ref[1]
    vectors, points = field.shape[1:]
    samples = samples_ref.shape[1]
    packed = weight_refs[0].shape[1]
    factors = []
    for c in range(blocks):
        head, tail, columns, grid = [], [], [], []
        for p in range(parts):
            grid.append(samples_ref[(zg ^ c) * parts + lax.rem(smp - p + parts, parts)])
            head.append(weight_refs[p][c, :samples, :])
            rest = weight_refs[p][c, samples:, :]
            tail += [rest[:, :64], rest[:, 64:]]
        extra = offers[c - 1][blocks * packed:, :] if c else extra_ref[...]
        extra = extra.astype(jnp.float32)
        for column in range(extra.shape[0] // 8):
            terms = extra[column * 8:column * 8 + 8]
            columns.append(terms[0:2] + terms[2:4] + terms[4:6])
        factors.append(jnp.concatenate(columns, axis=1))
        grid = jnp.concatenate(grid, axis=0)
        head = jnp.concatenate(head, axis=0)
        tail = jnp.concatenate(tail, axis=0)
        field[c, :128, :] = lax.dot_general(
            head, grid, (((0,), (0,)), ((), ())), preferred_element_type=jnp.float32
        )
        field[c, 128:, :] = lax.dot_general(
            tail, grid, (((0,), (0,)), ((), ())), preferred_element_type=jnp.float32
        )
    share = vectors // parts
    for p in range(parts):
        rows = slice(p * share, (p + 1) * share)
        level = [field[c, rows, :] for c in range(blocks)]
        for index, distance in enumerate((2, 1)):
            level = [
                level[c] + factors[c][index:index + 1, :] * level[c ^ distance]
                for c in range(blocks)
            ]
        for c in range(blocks):
            out_ref[(zg ^ c) * parts + p] = level[c].astype(jnp.bfloat16)


def exchange(pieces, axis, route):
    count = lax.axis_size(axis)
    came = {}
    for offset in sorted(pieces, key=lambda k: abs(k - count // 2)):
        pairs = [(i, route(i, offset) % count) for i in range(count)]
        came[offset] = lax.ppermute(pieces[offset], axis, pairs)
    return [came[offset] for offset in sorted(pieces)]


def body(forward_samples, adjoint_samples, probe_values, owners, block_ranks, twiddle):
    groups, parts = lax.axis_size("zg"), lax.axis_size("smp")
    y_count = lax.axis_size("y")
    samples, points = forward_samples.shape
    vectors = probe_values.shape[1]
    members = groups * parts
    piece = points // members
    smp = lax.axis_index("smp")
    y, core = lax.axis_index("y"), lax.axis_index("core")

    pieces = split(forward_samples, members)
    own, probes = owners.T, probe_values.T
    pieces, own = lax.optimization_barrier((pieces, own))
    pieces = lax.all_to_all(pieces, GROUP, 0, 0, tiled=True)

    wide = jnp.concatenate([probes, probes[128:]], axis=0)
    shape = (lax.axis_size(Z_AXES), samples * vectors // 128, 128)
    place = jnp.stack([y, core])

    def partial(offset, other, kind, *came):
        return local_call(
            lambda *refs: partial_kernel(y_count, offset, other, *refs),
            jax.ShapeDtypeStruct(shape, kind),
            place,
            own,
            adjoint_samples,
            wide,
            *came,
            smem=1,
            scratch=[pltpu.VMEM((shape[0] * samples, own.shape[1]), jnp.bfloat16)],
            flops=2 * shape[0] * samples * own.shape[1] * 256,
        )

    order = sorted(range(y_count), key=lambda k: (k == 0, abs(k - y_count // 2)))
    came = {}
    for offset in order:
        sent = partial(offset, True, jnp.float32)
        came[offset] = lax.ppermute(sent, "core", [(0, 1), (1, 0)])
    sums = []
    for offset in order:
        kind = jnp.bfloat16 if offset else jnp.float32
        merged = partial(offset, False, kind, came[offset])
        route = [(i, (i + offset) % y_count) for i in range(y_count)]
        sums.append(lax.ppermute(merged, "y", route) if offset else merged)
    sums = sums[-1:] + sums[:-1]
    shape = (groups,) + shape[1:]
    shapes = [jax.ShapeDtypeStruct(shape, jnp.float32), jax.ShapeDtypeStruct(shape, jnp.bfloat16)]
    zl = lax.axis_index("zl")
    kept, sent = local_call(halve_kernel, shapes, zl[None], *sums, smem=1)
    came = lax.ppermute(sent, "zl", [(0, 1), (1, 0)])
    tail = 8 * piece // shape[2]
    shapes = [jax.ShapeDtypeStruct(shape, jnp.float32)]
    shapes += [jax.ShapeDtypeStruct((tail, shape[2]), jnp.bfloat16)]
    offer = (groups * shape[1] + tail, shape[2])
    shapes += [jax.ShapeDtypeStruct(offer, jnp.bfloat16)] * (groups - 1)
    zg = lax.axis_index("zg")
    place = jnp.stack([zg, smp, block_ranks[0]])
    partial, extra, *offers = local_call(
        offer_kernel,
        shapes,
        place,
        kept,
        came,
        twiddle,
        smem=1,
        scratch=[pltpu.VMEM(shape, jnp.float32)],
    )
    *offers, pieces = lax.optimization_barrier((*offers, pieces))
    offers = exchange(dict(enumerate(offers, 1)), "zg", lambda i, k: i ^ k)
    weights = local_call(
        weights_kernel,
        jax.ShapeDtypeStruct(shape, jnp.bfloat16),
        place,
        partial,
        extra,
        *offers,
        smem=1,
    )
    others = exchange({p: weights for p in range(1, parts)}, "smp", lambda i, k: i + k)
    result = local_call(
        lambda *refs: field_kernel(groups, parts, *refs),
        jax.ShapeDtypeStruct((members, vectors // parts, piece), jnp.bfloat16),
        place,
        pieces,
        extra,
        *offers,
        weights,
        *others,
        smem=1,
        scratch=[pltpu.VMEM((groups, vectors, piece), jnp.float32)],
        flops=2 * members * samples * vectors * piece,
    )
    result = lax.all_to_all(result, GROUP, 0, 0, tiled=True)
    return result.transpose(1, 0, 2).reshape(vectors // parts, points)


def solution(mesh):
    grid = Mesh(mesh.devices.reshape(4, 2, 4, 2, 4), BLK + ("smp",))
    in_specs = (
        P("smp", BLK),
        P("smp", BLK),
        P(BLK, None),
        P(BLK, None),
        P(BLK),
        P(None, BLK),
    )
    out_specs = P("smp", BLK)
    return jax.shard_map(body, mesh=grid, in_specs=in_specs, out_specs=out_specs, check_vma=False)
```

```python
import jax
import jax.numpy as jnp
from jax import lax
from jax.experimental import pallas as pl
from jax.experimental.pallas import tpu as pltpu
from jax.sharding import Mesh, PartitionSpec as P

GROUP = ("zg", "smp")
Z_AXES = ("zg", "zl")
BLK = ("zg", "zl", "y", "core")
MIB = 1024 * 1024
VMEM = pl.BlockSpec(memory_space=pltpu.VMEM)
SMEM = pl.BlockSpec(memory_space=pltpu.SMEM)


def split_kernel(source_ref, out_ref, sems):
    pieces, _, points = out_ref.shape
    copies = [
        pltpu.make_async_copy(source_ref.at[:, pl.ds(i * points, points)], out_ref.at[i], sems.at[i])
        for i in range(pieces)
    ]
    for copy in copies:
        copy.start()
    for copy in copies:
        copy.wait()


def split(source, pieces):
    rows, points = source.shape
    return pl.pallas_call(
        split_kernel,
        out_shape=jax.ShapeDtypeStruct((pieces, rows, points // pieces), source.dtype),
        in_specs=[pl.BlockSpec(memory_space=pl.ANY)],
        out_specs=pl.BlockSpec(memory_space=pl.ANY),
        scratch_shapes=[pltpu.SemaphoreType.DMA((pieces,))],
        compiler_params=pltpu.CompilerParams(vmem_limit_bytes=56 * MIB),
        cost_estimate=pl.CostEstimate(flops=0, bytes_accessed=2 * MIB, transcendentals=0),
    )(source)


def join_kernel(parts, pieces_ref, out_ref, sems):
    pieces, _, points = pieces_ref.shape
    copies = []
    for i in range(pieces):
        place = (i % (pieces // parts)) * parts + i // (pieces // parts)
        target = out_ref.at[:, pl.ds(place * points, points)]
        copies.append(pltpu.make_async_copy(pieces_ref.at[i], target, sems.at[i]))
    for copy in copies:
        copy.start()
    for copy in copies:
        copy.wait()


def join(pieces, parts):
    count, rows, points = pieces.shape
    return pl.pallas_call(
        lambda *refs: join_kernel(parts, *refs),
        out_shape=jax.ShapeDtypeStruct((rows, count * points), pieces.dtype),
        in_specs=[VMEM],
        out_specs=pl.BlockSpec(memory_space=pl.ANY),
        scratch_shapes=[pltpu.SemaphoreType.DMA((count,))],
        compiler_params=pltpu.CompilerParams(vmem_limit_bytes=12 * MIB),
        cost_estimate=pl.CostEstimate(flops=0, bytes_accessed=2 * MIB, transcendentals=0),
    )(pieces)


def partial_kernel(y_count, offset, other, place_ref, owners_ref, adjoint_ref, probes_ref, *refs):
    out_ref, masked = refs[-2:]
    samples = adjoint_ref.shape[0]
    z_count = out_ref.shape[0]
    own = owners_ref[...]
    adjoint = adjoint_ref[...]
    y = lax.rem(place_ref[0] + offset, y_count)
    core = 1 - place_ref[1] if other else place_ref[1]
    for z in range(z_count):
        hot = jnp.where(own == (z * y_count + y) * 2 + core, 1.0, 0.0).astype(jnp.bfloat16)
        masked[z * samples:(z + 1) * samples, :] = adjoint * hot
    product = lax.dot_general(
        masked[...], probes_ref[...], (((1,), (1,)), ((), ())), preferred_element_type=jnp.float32
    )
    half = samples // 2
    for z in range(z_count):
        block = product[z * samples:(z + 1) * samples, :]
        head = block[:, :128]
        tail = jnp.concatenate([block[:half, 128:], block[half:, 128:]], axis=1)
        if not other:
            head = head + refs[0][z, :samples, :]
            tail = tail + refs[0][z, samples:, :]
        out_ref[z, :samples, :] = head.astype(out_ref.dtype)
        out_ref[z, samples:, :] = tail.astype(out_ref.dtype)


def local_call(kernel, out_shape, *args, smem=0, scratch=(), flops=0):
    return pl.pallas_call(
        kernel,
        out_shape=out_shape,
        in_specs=[SMEM] * smem + [VMEM] * (len(args) - smem),
        out_specs=jax.tree.map(lambda _: VMEM, out_shape),
        scratch_shapes=list(scratch),
        compiler_params=pltpu.CompilerParams(vmem_limit_bytes=12 * MIB),
        cost_estimate=pl.CostEstimate(flops=flops, bytes_accessed=2 * MIB, transcendentals=0),
    )(*args)


def halve_kernel(place_ref, *refs):
    kept_ref, sent_ref = refs[-2:]
    for block in range(kept_ref.shape[0]):
        for parity, out_ref in ((place_ref[0], kept_ref), (1 - place_ref[0], sent_ref)):
            z = block * 2 + parity
            total = refs[0][z]
            for ref in refs[1:-2]:
                total = total + ref[z].astype(jnp.float32)
            out_ref[block] = total.astype(out_ref.dtype)


def offer_kernel(place_ref, kept_ref, came_ref, twiddle_ref, own_ref, extra_ref, *refs):
    out_refs, total = refs[:-1], refs[-1]
    zg, smp, rank = place_ref[0], place_ref[1], place_ref[2]
    blocks, packed, lanes = kept_ref.shape
    levels, points = twiddle_ref.shape
    piece = points // (blocks * blocks)
    total[...] = kept_ref[...] + came_ref[...].astype(jnp.float32)
    rank = jnp.full((8 - 3 * levels, lanes), rank.astype(jnp.float32))
    for distance in range(blocks):
        partner = zg ^ distance
        start = (partner * blocks + smp) * piece
        rows = []
        for column in range(piece // lanes):
            left = twiddle_ref[:, pl.ds(pl.multiple_of(start + column * lanes, lanes), lanes)]
            for _ in range(3):
                term = left.astype(jnp.bfloat16).astype(jnp.float32)
                left = left - term
                rows.append(term)
            rows.append(rank)
        rows = jnp.concatenate(rows, axis=0).astype(jnp.bfloat16)
        for block in range(blocks):
            value = total[partner ^ block]
            if distance == 0:
                own_ref[block] = value
            else:
                target = slice(block * packed, (block + 1) * packed)
                out_refs[distance - 1][target, :] = value.astype(jnp.bfloat16)
        if distance == 0:
            extra_ref[...] = rows
        else:
            out_refs[distance - 1][blocks * packed:, :] = rows


def weights_kernel(place_ref, own_ref, extra_ref, *refs):
    offers, out_ref = refs[:-1], refs[-1]
    blocks, packed, lanes = own_ref.shape
    samples = packed * 2 // 3
    row = lax.broadcasted_iota(jnp.int32, (packed, lanes), 0)
    lane = lax.broadcasted_iota(jnp.int32, (packed, lanes), 1)
    tail = row - samples + jnp.where(lane < 64, 0, samples // 2)
    sample = place_ref[1] * samples + jnp.where(row < samples, row, tail)
    sample = sample.astype(jnp.float32)
    for block in range(blocks):
        total = own_ref[block]
        for offer in offers:
            total = total + offer[block * packed:(block + 1) * packed, :].astype(jnp.float32)
        extra = offers[block - 1][blocks * packed:, :] if block else extra_ref[...]
        rank = extra.astype(jnp.float32)[6:7]
        out_ref[block] = jnp.where(sample < rank, total, 0.0).astype(jnp.bfloat16)


def field_kernel(blocks, parts, place_ref, samples_ref, extra_ref, *refs):
    offers, weight_refs = refs[:blocks - 1], refs[blocks - 1:-3]
    out_ref, field, every = refs[-3:]
    zg, smp = place_ref[0], place_ref[1]
    vectors, points = field.shape[1:]
    samples = samples_ref.shape[1]
    packed = every.shape[2]
    for p in range(parts):
        every[lax.rem(smp - p + parts, parts)] = weight_refs[p][...]
    factors = []
    for c in range(blocks):
        head, tail, columns = [], [], []
        for p in range(parts):
            head.append(every[p, c, :samples, :])
            rest = every[p, c, samples:, :]
            tail += [rest[:, :64], rest[:, 64:]]
        extra = offers[c - 1][blocks * packed:, :] if c else extra_ref[...]
        extra = extra.astype(jnp.float32)
        for column in range(extra.shape[0] // 8):
            terms = extra[column * 8:column * 8 + 8]
            columns.append(terms[0:2] + terms[2:4] + terms[4:6])
        factors.append(jnp.concatenate(columns, axis=1))
        grid = samples_ref[pl.ds((zg ^ c) * parts, parts)].reshape(parts * samples, points)
        head = jnp.concatenate(head, axis=0)
        tail = jnp.concatenate(tail, axis=0)
        field[c, :128, :] = lax.dot_general(
            head, grid, (((0,), (0,)), ((), ())), preferred_element_type=jnp.float32
        )
        field[c, 128:, :] = lax.dot_general(
            tail, grid, (((0,), (0,)), ((), ())), preferred_element_type=jnp.float32
        )
    share = vectors // parts
    for p in range(parts):
        rows = slice(p * share, (p + 1) * share)
        level = [field[c, rows, :] for c in range(blocks)]
        for index, distance in enumerate((2, 1)):
            level = [
                level[c] + factors[c][index:index + 1, :] * level[c ^ distance]
                for c in range(blocks)
            ]
        for c in range(blocks):
            out_ref[p * blocks + (zg ^ c)] = level[c].astype(jnp.bfloat16)


def exchange(pieces, axis, route):
    count = lax.axis_size(axis)
    came = {}
    for offset in sorted(pieces, key=lambda k: abs(k - count // 2)):
        pairs = [(i, route(i, offset) % count) for i in range(count)]
        came[offset] = lax.ppermute(pieces[offset], axis, pairs)
    return [came[offset] for offset in sorted(pieces)]


def body(forward_samples, adjoint_samples, probe_values, owners, block_ranks, twiddle):
    groups, parts = lax.axis_size("zg"), lax.axis_size("smp")
    y_count = lax.axis_size("y")
    samples, points = forward_samples.shape
    vectors = probe_values.shape[1]
    members = groups * parts
    piece = points // members
    smp = lax.axis_index("smp")
    y, core = lax.axis_index("y"), lax.axis_index("core")

    pieces = split(forward_samples, members)
    own, probes = owners.T, probe_values.T
    pieces, own = lax.optimization_barrier((pieces, own))
    pieces = lax.all_to_all(pieces, GROUP, 0, 0, tiled=True)

    shape = (lax.axis_size(Z_AXES), samples * vectors // 128, 128)
    place = jnp.stack([y, core])

    def partial(offset, other, kind, *came):
        return local_call(
            lambda *refs: partial_kernel(y_count, offset, other, *refs),
            jax.ShapeDtypeStruct(shape, kind),
            place,
            own,
            adjoint_samples,
            probes,
            *came,
            smem=1,
            scratch=[pltpu.VMEM((shape[0] * samples, own.shape[1]), jnp.bfloat16)],
            flops=2 * shape[0] * samples * own.shape[1] * 256,
        )

    order = sorted(range(y_count), key=lambda k: (k == 0, abs(k - y_count // 2)))
    came, sums = {}, {}
    steps = [(offset, True) for offset in order[:-1]] + [(offset, False) for offset in order[:-1]]
    for offset, other in steps + [(0, True), (0, False)]:
        if other:
            sent = partial(offset, True, jnp.float32)
            came[offset] = lax.ppermute(sent, "core", [(0, 1), (1, 0)])
        elif offset:
            merged = partial(offset, False, jnp.bfloat16, came[offset])
            route = [(i, (i + offset) % y_count) for i in range(y_count)]
            sums[offset] = lax.ppermute(merged, "y", route)
        else:
            sums[offset] = partial(offset, False, jnp.float32, came[offset])
    sums = [sums[offset] for offset in range(y_count)]
    shape = (groups,) + shape[1:]
    shapes = [jax.ShapeDtypeStruct(shape, jnp.float32), jax.ShapeDtypeStruct(shape, jnp.bfloat16)]
    zl = lax.axis_index("zl")
    kept, sent = local_call(halve_kernel, shapes, zl[None], *sums, smem=1)
    came = lax.ppermute(sent, "zl", [(0, 1), (1, 0)])
    tail = 8 * piece // shape[2]
    shapes = [jax.ShapeDtypeStruct(shape, jnp.float32)]
    shapes += [jax.ShapeDtypeStruct((tail, shape[2]), jnp.bfloat16)]
    offer = (groups * shape[1] + tail, shape[2])
    shapes += [jax.ShapeDtypeStruct(offer, jnp.bfloat16)] * (groups - 1)
    zg = lax.axis_index("zg")
    place = jnp.stack([zg, smp, block_ranks[0]])
    partial, extra, *offers = local_call(
        offer_kernel,
        shapes,
        place,
        kept,
        came,
        twiddle,
        smem=1,
        scratch=[pltpu.VMEM(shape, jnp.float32)],
    )
    *offers, pieces = lax.optimization_barrier((*offers, pieces))
    offers = exchange(dict(enumerate(offers, 1)), "zg", lambda i, k: i ^ k)
    weights = local_call(
        weights_kernel,
        jax.ShapeDtypeStruct(shape, jnp.bfloat16),
        place,
        partial,
        extra,
        *offers,
        smem=1,
    )
    others = exchange({p: weights for p in range(1, parts)}, "smp", lambda i, k: i + k)
    result = local_call(
        lambda *refs: field_kernel(groups, parts, *refs),
        jax.ShapeDtypeStruct((members, vectors // parts, piece), jnp.bfloat16),
        place,
        pieces,
        extra,
        *offers,
        weights,
        *others,
        smem=1,
        scratch=[
            pltpu.VMEM((groups, vectors, piece), jnp.float32),
            pltpu.VMEM((parts,) + shape, jnp.bfloat16),
        ],
        flops=2 * members * samples * vectors * piece,
    )
    result = lax.all_to_all(result, ("smp", "zg"), 0, 0, tiled=True)
    return join(result, parts)


def solution(mesh):
    grid = Mesh(mesh.devices.reshape(4, 2, 4, 2, 4), BLK + ("smp",))
    in_specs = (
        P("smp", BLK),
        P("smp", BLK),
        P(BLK, None),
        P(BLK, None),
        P(BLK),
        P(None, BLK),
    )
    out_specs = P("smp", BLK)
    return jax.shard_map(body, mesh=grid, in_specs=in_specs, out_specs=out_specs, check_vma=False)
```

```python
import jax
import jax.numpy as jnp
from jax import lax
from jax.experimental import pallas as pl
from jax.experimental.pallas import tpu as pltpu
from jax.sharding import Mesh, PartitionSpec as P

GROUP = ("zg", "smp")
Z_AXES = ("zg", "zl")
BLK = ("zg", "zl", "y", "core")
MIB = 1024 * 1024
VMEM = pl.BlockSpec(memory_space=pltpu.VMEM)
SMEM = pl.BlockSpec(memory_space=pltpu.SMEM)


def split_kernel(source_ref, out_ref):
    points = out_ref.shape[2]
    for i in range(out_ref.shape[0]):
        out_ref[i] = source_ref[:, i * points:(i + 1) * points]


def split(source, pieces):
    rows, points = source.shape
    steps = 4
    return pl.pallas_call(
        split_kernel,
        grid=(steps,),
        out_shape=jax.ShapeDtypeStruct((pieces, rows, points // pieces), source.dtype),
        in_specs=[pl.BlockSpec((rows, points // steps), lambda i: (0, i))],
        out_specs=pl.BlockSpec((pieces // steps, rows, points // pieces), lambda i: (i, 0, 0)),
        compiler_params=pltpu.CompilerParams(vmem_limit_bytes=56 * MIB),
        cost_estimate=pl.CostEstimate(flops=0, bytes_accessed=2 * MIB, transcendentals=0),
    )(source)


def partial_kernel(y_count, offsets, other, place_ref, owners_ref, adjoint_ref, probes_ref, *refs):
    out_ref, masked = refs
    step = pl.program_id(0)
    samples = adjoint_ref.shape[0]
    z_count = out_ref.shape[1]
    own = owners_ref[...]
    adjoint = adjoint_ref[...]
    offset = offsets[-1]
    for i, value in enumerate(offsets[:-1]):
        offset = jnp.where(step == i, value, offset)
    y = lax.rem(place_ref[0] + offset, y_count)
    core = 1 - place_ref[1] if other else place_ref[1]
    for z in range(z_count):
        hot = jnp.where(own == (z * y_count + y) * 2 + core, 1.0, 0.0).astype(jnp.bfloat16)
        masked[z * samples:(z + 1) * samples, :] = adjoint * hot
    product = lax.dot_general(
        masked[...], probes_ref[...], (((1,), (1,)), ((), ())), preferred_element_type=jnp.float32
    )
    half = samples // 2
    for z in range(z_count):
        block = product[z * samples:(z + 1) * samples, :]
        out_ref[0, z, :samples, :] = block[:, :128]
        tail = jnp.concatenate([block[:half, 128:], block[half:, 128:]], axis=1)
        out_ref[0, z, samples:, :] = tail


def partial_coeffs(offsets, other, place, owners, adjoint, probes):
    samples, rows = adjoint.shape
    vectors = probes.shape[0]
    y_count, z_count = lax.axis_size("y"), lax.axis_size(Z_AXES)
    shape = (len(offsets), z_count, samples * vectors // 128, 128)
    return pl.pallas_call(
        lambda *refs: partial_kernel(y_count, offsets, other, *refs),
        grid=(len(offsets),),
        in_specs=[
            SMEM,
            pl.BlockSpec((1, rows), lambda i: (0, 0)),
            pl.BlockSpec((samples, rows), lambda i: (0, 0)),
            pl.BlockSpec((vectors, rows), lambda i: (0, 0)),
        ],
        out_specs=pl.BlockSpec((1,) + shape[1:], lambda i: (i, 0, 0, 0)),
        out_shape=jax.ShapeDtypeStruct(shape, jnp.float32),
        scratch_shapes=[pltpu.VMEM((z_count * samples, rows), jnp.bfloat16)],
        compiler_params=pltpu.CompilerParams(vmem_limit_bytes=12 * MIB),
        cost_estimate=pl.CostEstimate(
            flops=2 * len(offsets) * z_count * samples * rows * 256,
            bytes_accessed=3 * MIB,
            transcendentals=0,
        ),
    )(place, owners, adjoint, probes)


def local_call(kernel, out_shape, *args, smem=0, scratch=(), flops=0):
    return pl.pallas_call(
        kernel,
        out_shape=out_shape,
        in_specs=[SMEM] * smem + [VMEM] * (len(args) - smem),
        out_specs=jax.tree.map(lambda _: VMEM, out_shape),
        scratch_shapes=list(scratch),
        compiler_params=pltpu.CompilerParams(vmem_limit_bytes=12 * MIB),
        cost_estimate=pl.CostEstimate(flops=flops, bytes_accessed=2 * MIB, transcendentals=0),
    )(*args)


def merge_kernel(kept_ref, came_ref, *out_refs):
    for i, out_ref in enumerate(out_refs):
        out_ref[...] = (kept_ref[i] + came_ref[i]).astype(out_ref.dtype)


def halve_kernel(place_ref, *refs):
    kept_ref, sent_ref = refs[-2:]
    for block in range(kept_ref.shape[0]):
        for parity, out_ref in ((place_ref[0], kept_ref), (1 - place_ref[0], sent_ref)):
            z = block * 2 + parity
            total = refs[0][z]
            for ref in refs[1:-2]:
                total = total + ref[z].astype(jnp.float32)
            out_ref[block] = total.astype(out_ref.dtype)


def offer_kernel(place_ref, kept_ref, came_ref, twiddle_ref, own_ref, extra_ref, *refs):
    out_refs, total = refs[:-1], refs[-1]
    zg, smp, rank = place_ref[0], place_ref[1], place_ref[2]
    blocks, packed, lanes = kept_ref.shape
    levels, points = twiddle_ref.shape
    piece = points // (blocks * blocks)
    total[...] = kept_ref[...] + came_ref[...].astype(jnp.float32)
    rank = jnp.full((8 - 3 * levels, lanes), rank.astype(jnp.float32))
    for distance in range(blocks):
        partner = zg ^ distance
        start = (partner * blocks + smp) * piece
        rows = []
        for column in range(piece // lanes):
            left = twiddle_ref[:, pl.ds(pl.multiple_of(start + column * lanes, lanes), lanes)]
            for _ in range(3):
                term = left.astype(jnp.bfloat16).astype(jnp.float32)
                left = left - term
                rows.append(term)
            rows.append(rank)
        rows = jnp.concatenate(rows, axis=0).astype(jnp.bfloat16)
        for block in range(blocks):
            value = total[partner ^ block]
            if distance == 0:
                own_ref[block] = value
            else:
                target = slice(block * packed, (block + 1) * packed)
                out_refs[distance - 1][target, :] = value.astype(jnp.bfloat16)
        if distance == 0:
            extra_ref[...] = rows
        else:
            out_refs[distance - 1][blocks * packed:, :] = rows


def weights_kernel(place_ref, own_ref, extra_ref, *refs):
    offers, (out_ref, rows_ref) = refs[:-2], refs[-2:]
    blocks, packed, lanes = own_ref.shape
    samples = packed * 2 // 3
    row = lax.broadcasted_iota(jnp.int32, (packed, lanes), 0)
    lane = lax.broadcasted_iota(jnp.int32, (packed, lanes), 1)
    tail = row - samples + jnp.where(lane < 64, 0, samples // 2)
    sample = place_ref[1] * samples + jnp.where(row < samples, row, tail)
    sample = sample.astype(jnp.float32)
    for block in range(blocks):
        total = own_ref[block]
        for offer in offers:
            total = total + offer[block * packed:(block + 1) * packed, :].astype(jnp.float32)
        extra = offers[block - 1][blocks * packed:, :] if block else extra_ref[...]
        rows_ref[block] = extra
        rank = extra.astype(jnp.float32)[6:7]
        out_ref[block] = jnp.where(sample < rank, total, 0.0).astype(jnp.bfloat16)


def field_kernel(blocks, parts, place_ref, samples_ref, rows_ref, *refs):
    weight_refs = refs[:-3]
    out_ref, field, every = refs[-3:]
    zg, smp = place_ref[0], place_ref[1]
    vectors, points = field.shape[1:]
    samples = samples_ref.shape[1]
    for p in range(parts):
        every[lax.rem(smp - p + parts, parts)] = weight_refs[p][...]
    factors = []
    for c in range(blocks):
        head, tail, columns = [], [], []
        for p in range(parts):
            head.append(every[p, c, :samples, :])
            rest = every[p, c, samples:, :]
            tail += [rest[:, :64], rest[:, 64:]]
        extra = rows_ref[c].astype(jnp.float32)
        for column in range(extra.shape[0] // 8):
            terms = extra[column * 8:column * 8 + 8]
            columns.append(terms[0:2] + terms[2:4] + terms[4:6])
        factors.append(jnp.concatenate(columns, axis=1))
        grid = samples_ref[pl.ds((zg ^ c) * parts, parts)].reshape(parts * samples, points)
        head = jnp.concatenate(head, axis=0)
        tail = jnp.concatenate(tail, axis=0)
        field[c, :128, :] = lax.dot_general(
            head, grid, (((0,), (0,)), ((), ())), preferred_element_type=jnp.float32
        )
        field[c, 128:, :] = lax.dot_general(
            tail, grid, (((0,), (0,)), ((), ())), preferred_element_type=jnp.float32
        )
    share = vectors // parts
    for p in range(parts):
        rows = slice(p * share, (p + 1) * share)
        level = [field[c, rows, :] for c in range(blocks)]
        for index, distance in enumerate((2, 1)):
            level = [
                level[c] + factors[c][index:index + 1, :] * level[c ^ distance]
                for c in range(blocks)
            ]
        for c in range(blocks):
            out_ref[(zg ^ c) * parts + p] = level[c].astype(jnp.bfloat16)


def exchange(pieces, axis, route):
    count = lax.axis_size(axis)
    came = {}
    for offset in sorted(pieces, key=lambda k: abs(k - count // 2)):
        pairs = [(i, route(i, offset) % count) for i in range(count)]
        came[offset] = lax.ppermute(pieces[offset], axis, pairs)
    return [came[offset] for offset in sorted(pieces)]


def body(forward_samples, adjoint_samples, probe_values, owners, block_ranks, twiddle):
    groups, parts = lax.axis_size("zg"), lax.axis_size("smp")
    y_count = lax.axis_size("y")
    samples, points = forward_samples.shape
    vectors = probe_values.shape[1]
    members = groups * parts
    piece = points // members
    smp = lax.axis_index("smp")
    y, core = lax.axis_index("y"), lax.axis_index("core")

    pieces = split(forward_samples, members)
    own, probes = owners.T, probe_values.T
    pieces, own = lax.optimization_barrier((pieces, own))
    pieces = lax.all_to_all(pieces, GROUP, 0, 0, tiled=True)

    place = jnp.stack([y, core])
    order = sorted(range(y_count), key=lambda k: (k == 0, abs(k - y_count // 2)))
    sent = partial_coeffs(order, True, place, own, adjoint_samples, probes)
    came = lax.ppermute(sent, "core", [(0, 1), (1, 0)])
    shape = sent.shape[1:]
    kept = partial_coeffs(order, False, place, own, adjoint_samples, probes)
    kinds = [jnp.bfloat16 if offset else jnp.float32 for offset in order]
    merged = local_call(
        merge_kernel, [jax.ShapeDtypeStruct(shape, kind) for kind in kinds], kept, came
    )
    sums = {}
    for offset, value in zip(order, merged):
        route = [(i, (i + offset) % y_count) for i in range(y_count)]
        sums[offset] = lax.ppermute(value, "y", route) if offset else value
    sums = [sums[offset] for offset in range(y_count)]
    shape = (groups,) + shape[1:]
    shapes = [jax.ShapeDtypeStruct(shape, jnp.float32), jax.ShapeDtypeStruct(shape, jnp.bfloat16)]
    zl = lax.axis_index("zl")
    kept, sent = local_call(halve_kernel, shapes, zl[None], *sums, smem=1)
    came = lax.ppermute(sent, "zl", [(0, 1), (1, 0)])
    tail = 8 * piece // shape[2]
    shapes = [jax.ShapeDtypeStruct(shape, jnp.float32)]
    shapes += [jax.ShapeDtypeStruct((tail, shape[2]), jnp.bfloat16)]
    offer = (groups * shape[1] + tail, shape[2])
    shapes += [jax.ShapeDtypeStruct(offer, jnp.bfloat16)] * (groups - 1)
    zg = lax.axis_index("zg")
    place = jnp.stack([zg, smp, block_ranks[0]])
    partial, extra, *offers = local_call(
        offer_kernel,
        shapes,
        place,
        kept,
        came,
        twiddle,
        smem=1,
        scratch=[pltpu.VMEM(shape, jnp.float32)],
    )
    *offers, pieces = lax.optimization_barrier((*offers, pieces))
    offers = exchange(dict(enumerate(offers, 1)), "zg", lambda i, k: i ^ k)
    shapes = [jax.ShapeDtypeStruct(shape, jnp.bfloat16)]
    shapes += [jax.ShapeDtypeStruct((groups,) + extra.shape, jnp.bfloat16)]
    weights, factors = local_call(
        weights_kernel,
        shapes,
        place,
        partial,
        extra,
        *offers,
        smem=1,
    )
    others = exchange({p: weights for p in range(1, parts)}, "smp", lambda i, k: i + k)
    result = local_call(
        lambda *refs: field_kernel(groups, parts, *refs),
        jax.ShapeDtypeStruct((members, vectors // parts, piece), jnp.bfloat16),
        place,
        pieces,
        factors,
        weights,
        *others,
        smem=1,
        scratch=[
            pltpu.VMEM((groups, vectors, piece), jnp.float32),
            pltpu.VMEM((parts,) + shape, jnp.bfloat16),
        ],
        flops=2 * members * samples * vectors * piece,
    )
    result = lax.all_to_all(result, GROUP, 0, 0, tiled=True)
    return result.transpose(1, 0, 2).reshape(vectors // parts, points)


def solution(mesh):
    grid = Mesh(mesh.devices.reshape(4, 2, 4, 2, 4), BLK + ("smp",))
    in_specs = (
        P("smp", BLK),
        P("smp", BLK),
        P(BLK, None),
        P(BLK, None),
        P(BLK),
        P(None, BLK),
    )
    out_specs = P("smp", BLK)
    return jax.shard_map(body, mesh=grid, in_specs=in_specs, out_specs=out_specs, check_vma=False)
```

```python
import jax
import jax.numpy as jnp
from jax import lax
from jax.experimental import pallas as pl
from jax.experimental.pallas import tpu as pltpu
from jax.sharding import Mesh, PartitionSpec as P

GROUP = ("zg", "smp")
Z_AXES = ("zg", "zl")
BLK = ("zg", "zl", "y", "core")
MIB = 1024 * 1024
VMEM = pl.BlockSpec(memory_space=pltpu.VMEM)
SMEM = pl.BlockSpec(memory_space=pltpu.SMEM)


def partial_kernel(y_count, offset, place_ref, *refs):
    out_ref, masked = refs[-2:]
    z_count = out_ref.shape[0]
    y = lax.rem(place_ref[0] + offset, y_count)
    product = None
    for owners_ref, adjoint_ref, probes_ref in (refs[0:3], refs[3:6]):
        own = owners_ref[...]
        adjoint = adjoint_ref[...]
        samples = adjoint.shape[0]
        for z in range(z_count):
            owner = (z * y_count + y) * 2 + place_ref[1]
            hot = jnp.where(own == owner, 1.0, 0.0).astype(jnp.bfloat16)
            masked[z * samples:(z + 1) * samples, :] = adjoint * hot
        term = lax.dot_general(
            masked[...],
            probes_ref[...],
            (((1,), (1,)), ((), ())),
            preferred_element_type=jnp.float32,
        )
        product = term if product is None else product + term
    half = samples // 2
    for z in range(z_count):
        block = product[z * samples:(z + 1) * samples, :]
        tail = jnp.concatenate([block[:half, 128:], block[half:, 128:]], axis=1)
        out_ref[z, :samples, :] = block[:, :128].astype(out_ref.dtype)
        out_ref[z, samples:, :] = tail.astype(out_ref.dtype)


def local_call(kernel, out_shape, *args, smem=0, scratch=(), flops=0, moved=2 * MIB):
    return pl.pallas_call(
        kernel,
        out_shape=out_shape,
        in_specs=[SMEM] * smem + [VMEM] * (len(args) - smem),
        out_specs=jax.tree.map(lambda _: VMEM, out_shape),
        scratch_shapes=list(scratch),
        compiler_params=pltpu.CompilerParams(vmem_limit_bytes=12 * MIB),
        cost_estimate=pl.CostEstimate(flops=flops, bytes_accessed=moved, transcendentals=0),
    )(*args)


def halve_kernel(place_ref, *refs):
    kept_ref, sent_ref = refs[-2:]
    for block in range(kept_ref.shape[0]):
        for parity, out_ref in ((place_ref[0], kept_ref), (1 - place_ref[0], sent_ref)):
            z = block * 2 + parity
            total = refs[0][z]
            for ref in refs[1:-2]:
                total = total + ref[z].astype(jnp.float32)
            out_ref[block] = total.astype(out_ref.dtype)


def offer_kernel(place_ref, kept_ref, came_ref, twiddle_ref, own_ref, extra_ref, *refs):
    out_refs, total = refs[:-1], refs[-1]
    zg, smp, rank = place_ref[0], place_ref[1], place_ref[2]
    blocks, packed, lanes = kept_ref.shape
    levels, points = twiddle_ref.shape
    piece = points // (blocks * blocks)
    total[...] = kept_ref[...] + came_ref[...].astype(jnp.float32)
    rank = jnp.full((8 - 3 * levels, lanes), rank.astype(jnp.float32))
    for distance in range(blocks):
        partner = zg ^ distance
        start = (partner * blocks + smp) * piece
        rows = []
        for column in range(piece // lanes):
            left = twiddle_ref[:, pl.ds(pl.multiple_of(start + column * lanes, lanes), lanes)]
            for _ in range(3):
                term = left.astype(jnp.bfloat16).astype(jnp.float32)
                left = left - term
                rows.append(term)
            rows.append(rank)
        rows = jnp.concatenate(rows, axis=0).astype(jnp.bfloat16)
        for block in range(blocks):
            value = total[partner ^ block]
            if distance == 0:
                own_ref[block] = value
            else:
                target = slice(block * packed, (block + 1) * packed)
                out_refs[distance - 1][target, :] = value.astype(jnp.bfloat16)
        if distance == 0:
            extra_ref[...] = rows
        else:
            out_refs[distance - 1][blocks * packed:, :] = rows


def weights_kernel(place_ref, own_ref, extra_ref, *refs):
    offers, (out_ref, rows_ref) = refs[:-2], refs[-2:]
    blocks, packed, lanes = own_ref.shape
    samples = packed * 2 // 3
    row = lax.broadcasted_iota(jnp.int32, (packed, lanes), 0)
    lane = lax.broadcasted_iota(jnp.int32, (packed, lanes), 1)
    tail = row - samples + jnp.where(lane < 64, 0, samples // 2)
    sample = place_ref[1] * samples + jnp.where(row < samples, row, tail)
    sample = sample.astype(jnp.float32)
    for block in range(blocks):
        total = own_ref[block]
        for offer in offers:
            total = total + offer[block * packed:(block + 1) * packed, :].astype(jnp.float32)
        extra = offers[block - 1][blocks * packed:, :] if block else extra_ref[...]
        rows_ref[block] = extra
        rank = extra.astype(jnp.float32)[6:7]
        out_ref[block] = jnp.where(sample < rank, total, 0.0).astype(jnp.bfloat16)


def field_kernel(blocks, parts, place_ref, samples_ref, rows_ref, *refs):
    weight_refs = refs[:-3]
    out_ref, field, every = refs[-3:]
    zg, smp = place_ref[0], place_ref[1]
    vectors, points = field.shape[1:]
    samples = samples_ref.shape[1]
    for p in range(parts):
        every[lax.rem(smp - p + parts, parts)] = weight_refs[p][...]
    factors = []
    for c in range(blocks):
        head, tail, columns = [], [], []
        for p in range(parts):
            head.append(every[p, c, :samples, :])
            rest = every[p, c, samples:, :]
            tail += [rest[:, :64], rest[:, 64:]]
        extra = rows_ref[c].astype(jnp.float32)
        for column in range(extra.shape[0] // 8):
            terms = extra[column * 8:column * 8 + 8]
            columns.append(terms[0:2] + terms[2:4] + terms[4:6])
        factors.append(jnp.concatenate(columns, axis=1))
        grid = samples_ref[pl.ds((zg ^ c) * parts, parts)].reshape(parts * samples, points)
        head = jnp.concatenate(head, axis=0)
        tail = jnp.concatenate(tail, axis=0)
        field[c, :128, :] = lax.dot_general(
            head, grid, (((0,), (0,)), ((), ())), preferred_element_type=jnp.float32
        )
        field[c, 128:, :] = lax.dot_general(
            tail, grid, (((0,), (0,)), ((), ())), preferred_element_type=jnp.float32
        )
    share = vectors // parts
    for p in range(parts):
        rows = slice(p * share, (p + 1) * share)
        level = [field[c, rows, :] for c in range(blocks)]
        for index, distance in enumerate((2, 1)):
            level = [
                level[c] + factors[c][index:index + 1, :] * level[c ^ distance]
                for c in range(blocks)
            ]
        for c in range(blocks):
            out_ref[(zg ^ c) * parts + p] = level[c].astype(jnp.bfloat16)


def exchange(pieces, axis, route):
    count = lax.axis_size(axis)
    came = {}
    for offset in sorted(pieces, key=lambda k: abs(k - count // 2)):
        pairs = [(i, route(i, offset) % count) for i in range(count)]
        came[offset] = lax.ppermute(pieces[offset], axis, pairs)
    return [came[offset] for offset in sorted(pieces)]


def body(forward_samples, adjoint_samples, probe_values, owners, block_ranks, twiddle):
    groups, parts = lax.axis_size("zg"), lax.axis_size("smp")
    y_count = lax.axis_size("y")
    samples, points = forward_samples.shape
    vectors = probe_values.shape[1]
    members = groups * parts
    piece = points // members
    smp = lax.axis_index("smp")
    y, core = lax.axis_index("y"), lax.axis_index("core")

    pieces = forward_samples.reshape(samples, members, piece).transpose(1, 0, 2)
    own, probes = owners.T, probe_values.T
    rows = (own, adjoint_samples, probes)
    came = [lax.ppermute(x, "core", [(0, 1), (1, 0)]) for x in rows]
    pieces, *came = lax.optimization_barrier((pieces, *came))
    rows = (own, adjoint_samples, probes, *came)
    pieces = lax.all_to_all(pieces, GROUP, 0, 0, tiled=True)

    place = jnp.stack([y, core])
    shape = (lax.axis_size(Z_AXES), samples * vectors // 128, 128)
    sums = {}
    for offset in sorted(range(y_count), key=lambda k: (k == 0, abs(k - y_count // 2))):
        value = local_call(
            lambda *refs, offset=offset: partial_kernel(y_count, offset, *refs),
            jax.ShapeDtypeStruct(shape, jnp.bfloat16 if offset else jnp.float32),
            place,
            *rows,
            smem=1,
            scratch=[pltpu.VMEM((shape[0] * samples, own.shape[1]), jnp.bfloat16)],
            flops=16 * shape[0] * samples * own.shape[1] * 256,
        )
        route = [(i, (i + offset) % y_count) for i in range(y_count)]
        sums[offset] = lax.ppermute(value, "y", route) if offset else value
    sums = [sums[offset] for offset in range(y_count)]
    shape = (groups,) + shape[1:]
    shapes = [jax.ShapeDtypeStruct(shape, jnp.float32), jax.ShapeDtypeStruct(shape, jnp.bfloat16)]
    zl = lax.axis_index("zl")
    kept, sent = local_call(halve_kernel, shapes, zl[None], *sums, smem=1)
    came = lax.ppermute(sent, "zl", [(0, 1), (1, 0)])
    tail = 8 * piece // shape[2]
    shapes = [jax.ShapeDtypeStruct(shape, jnp.float32)]
    shapes += [jax.ShapeDtypeStruct((tail, shape[2]), jnp.bfloat16)]
    offer = (groups * shape[1] + tail, shape[2])
    shapes += [jax.ShapeDtypeStruct(offer, jnp.bfloat16)] * (groups - 1)
    zg = lax.axis_index("zg")
    place = jnp.stack([zg, smp, block_ranks[0]])
    partial, extra, *offers = local_call(
        offer_kernel,
        shapes,
        place,
        kept,
        came,
        twiddle,
        smem=1,
        scratch=[pltpu.VMEM(shape, jnp.float32)],
    )
    *offers, pieces = lax.optimization_barrier((*offers, pieces))
    offers = exchange(dict(enumerate(offers, 1)), "zg", lambda i, k: i ^ k)
    shapes = [jax.ShapeDtypeStruct(shape, jnp.bfloat16)]
    shapes += [jax.ShapeDtypeStruct((groups,) + extra.shape, jnp.bfloat16)]
    weights, factors = local_call(
        weights_kernel,
        shapes,
        place,
        partial,
        extra,
        *offers,
        smem=1,
    )
    others = exchange({p: weights for p in range(1, parts)}, "smp", lambda i, k: i + k)
    result = local_call(
        lambda *refs: field_kernel(groups, parts, *refs),
        jax.ShapeDtypeStruct((members, vectors // parts, piece), jnp.bfloat16),
        place,
        pieces,
        factors,
        weights,
        *others,
        smem=1,
        scratch=[
            pltpu.VMEM((groups, vectors, piece), jnp.float32),
            pltpu.VMEM((parts,) + shape, jnp.bfloat16),
        ],
        flops=2 * members * samples * vectors * piece,
    )
    result = lax.all_to_all(result, GROUP, 0, 0, tiled=True)
    return result.transpose(1, 0, 2).reshape(vectors // parts, points)


def solution(mesh):
    grid = Mesh(mesh.devices.reshape(4, 2, 4, 2, 4), BLK + ("smp",))
    in_specs = (
        P("smp", BLK),
        P("smp", BLK),
        P(BLK, None),
        P(BLK, None),
        P(BLK),
        P(None, BLK),
    )
    out_specs = P("smp", BLK)
    return jax.shard_map(body, mesh=grid, in_specs=in_specs, out_specs=out_specs, check_vma=False)
```

```python
import jax
import jax.numpy as jnp
from jax import lax
from jax.experimental import pallas as pl
from jax.experimental.pallas import tpu as pltpu
from jax.sharding import Mesh, PartitionSpec as P

GROUP = ("zg", "smp")
Z_AXES = ("zg", "zl")
BLK = ("zg", "zl", "y", "core")
MIB = 1024 * 1024
VMEM = pl.BlockSpec(memory_space=pltpu.VMEM)
SMEM = pl.BlockSpec(memory_space=pltpu.SMEM)


def partial_kernel(y_count, offset, place_ref, *refs):
    out_ref, masked = refs[-2:]
    z_count = out_ref.shape[0]
    y = lax.rem(place_ref[0] + offset, y_count)
    product = None
    for owners_ref, adjoint_ref, probes_ref in (refs[0:3], refs[3:6]):
        own = owners_ref[...]
        adjoint = adjoint_ref[...]
        samples = adjoint.shape[0]
        for z in range(z_count):
            owner = (z * y_count + y) * 2 + place_ref[1]
            hot = jnp.where(own == owner, 1.0, 0.0).astype(jnp.bfloat16)
            masked[z * samples:(z + 1) * samples, :] = adjoint * hot
        term = lax.dot_general(
            masked[...],
            probes_ref[...],
            (((1,), (1,)), ((), ())),
            preferred_element_type=jnp.float32,
        )
        product = term if product is None else product + term
    half = samples // 2
    for z in range(z_count):
        block = product[z * samples:(z + 1) * samples, :]
        tail = jnp.concatenate([block[:half, 128:], block[half:, 128:]], axis=1)
        out_ref[z, :samples, :] = block[:, :128].astype(out_ref.dtype)
        out_ref[z, samples:, :] = tail.astype(out_ref.dtype)


def local_call(kernel, out_shape, *args, smem=0, scratch=(), flops=0, moved=2 * MIB):
    return pl.pallas_call(
        kernel,
        out_shape=out_shape,
        in_specs=[SMEM] * smem + [VMEM] * (len(args) - smem),
        out_specs=jax.tree.map(lambda _: VMEM, out_shape),
        scratch_shapes=list(scratch),
        compiler_params=pltpu.CompilerParams(vmem_limit_bytes=12 * MIB),
        cost_estimate=pl.CostEstimate(flops=flops, bytes_accessed=moved, transcendentals=0),
    )(*args)


def join_kernel(place_ref, pieces_ref, out_ref, sems):
    count, _, points = pieces_ref.shape
    copies = []
    for i in range(count):
        place = jnp.where(place_ref[3] == 1, count - 1 - i, i)
        target = out_ref.at[:, pl.ds(pl.multiple_of(place * points, points), points)]
        copies.append(pltpu.make_async_copy(pieces_ref.at[i], target, sems.at[i]))
    for copy in copies:
        copy.start()
    for copy in copies:
        copy.wait()


def join(place, pieces):
    count, rows, points = pieces.shape
    return pl.pallas_call(
        join_kernel,
        out_shape=jax.ShapeDtypeStruct((rows, count * points), pieces.dtype),
        in_specs=[SMEM, VMEM],
        out_specs=pl.BlockSpec(memory_space=pl.ANY),
        scratch_shapes=[pltpu.SemaphoreType.DMA((count,))],
        compiler_params=pltpu.CompilerParams(vmem_limit_bytes=12 * MIB),
        cost_estimate=pl.CostEstimate(flops=0, bytes_accessed=2 * MIB, transcendentals=0),
    )(place, pieces)


def reversed_groups(zg, zl, y, core, smp):
    groups = []
    for rest in range(zl * y * core):
        members = [((g * zl * y * core) + rest) * smp + p for g in range(zg) for p in range(smp)]
        groups.append(members[::-1] if rest % core else members)
    return groups


def halve_kernel(place_ref, *refs):
    kept_ref, sent_ref = refs[-2:]
    for block in range(kept_ref.shape[0]):
        for parity, out_ref in ((place_ref[0], kept_ref), (1 - place_ref[0], sent_ref)):
            z = block * 2 + parity
            total = refs[0][z]
            for ref in refs[1:-2]:
                total = total + ref[z].astype(jnp.float32)
            out_ref[block] = total.astype(out_ref.dtype)


def offer_kernel(place_ref, kept_ref, came_ref, twiddle_ref, own_ref, extra_ref, *refs):
    out_refs, total = refs[:-1], refs[-1]
    zg, smp, rank = place_ref[0], place_ref[1], place_ref[2]
    blocks, packed, lanes = kept_ref.shape
    levels, points = twiddle_ref.shape
    piece = points // (blocks * blocks)
    total[...] = kept_ref[...] + came_ref[...].astype(jnp.float32)
    rank = jnp.full((8 - 3 * levels, lanes), rank.astype(jnp.float32))
    for distance in range(blocks):
        partner = zg ^ distance
        start = (partner * blocks + smp) * piece
        rows = []
        for column in range(piece // lanes):
            left = twiddle_ref[:, pl.ds(pl.multiple_of(start + column * lanes, lanes), lanes)]
            for _ in range(3):
                term = left.astype(jnp.bfloat16).astype(jnp.float32)
                left = left - term
                rows.append(term)
            rows.append(rank)
        rows = jnp.concatenate(rows, axis=0).astype(jnp.bfloat16)
        for block in range(blocks):
            value = total[partner ^ block]
            if distance == 0:
                own_ref[block] = value
            else:
                target = slice(block * packed, (block + 1) * packed)
                out_refs[distance - 1][target, :] = value.astype(jnp.bfloat16)
        if distance == 0:
            extra_ref[...] = rows
        else:
            out_refs[distance - 1][blocks * packed:, :] = rows


def weights_kernel(place_ref, own_ref, extra_ref, *refs):
    offers, (out_ref, rows_ref) = refs[:-2], refs[-2:]
    blocks, packed, lanes = own_ref.shape
    samples = packed * 2 // 3
    row = lax.broadcasted_iota(jnp.int32, (packed, lanes), 0)
    lane = lax.broadcasted_iota(jnp.int32, (packed, lanes), 1)
    tail = row - samples + jnp.where(lane < 64, 0, samples // 2)
    sample = place_ref[1] * samples + jnp.where(row < samples, row, tail)
    sample = sample.astype(jnp.float32)
    for block in range(blocks):
        total = own_ref[block]
        for offer in offers:
            total = total + offer[block * packed:(block + 1) * packed, :].astype(jnp.float32)
        extra = offers[block - 1][blocks * packed:, :] if block else extra_ref[...]
        rows_ref[block] = extra
        rank = extra.astype(jnp.float32)[6:7]
        out_ref[block] = jnp.where(sample < rank, total, 0.0).astype(jnp.bfloat16)


def field_kernel(blocks, parts, place_ref, samples_ref, rows_ref, *refs):
    weight_refs = refs[:-3]
    out_ref, field, every = refs[-3:]
    zg, smp = place_ref[0], place_ref[1]
    vectors, points = field.shape[1:]
    samples = samples_ref.shape[1]
    for p in range(parts):
        every[lax.rem(smp - p + parts, parts)] = weight_refs[p][...]
    factors = []
    for c in range(blocks):
        head, tail, columns = [], [], []
        for p in range(parts):
            head.append(every[p, c, :samples, :])
            rest = every[p, c, samples:, :]
            tail += [rest[:, :64], rest[:, 64:]]
        extra = rows_ref[c].astype(jnp.float32)
        for column in range(extra.shape[0] // 8):
            terms = extra[column * 8:column * 8 + 8]
            columns.append(terms[0:2] + terms[2:4] + terms[4:6])
        factors.append(jnp.concatenate(columns, axis=1))
        grid = samples_ref[pl.ds((zg ^ c) * parts, parts)].reshape(parts * samples, points)
        head = jnp.concatenate(head, axis=0)
        tail = jnp.concatenate(tail, axis=0)
        field[c, :128, :] = lax.dot_general(
            head, grid, (((0,), (0,)), ((), ())), preferred_element_type=jnp.float32
        )
        field[c, 128:, :] = lax.dot_general(
            tail, grid, (((0,), (0,)), ((), ())), preferred_element_type=jnp.float32
        )
    share = vectors // parts
    for p in range(parts):
        rows = slice(p * share, (p + 1) * share)
        level = [field[c, rows, :] for c in range(blocks)]
        for index, distance in enumerate((2, 1)):
            level = [
                level[c] + factors[c][index:index + 1, :] * level[c ^ distance]
                for c in range(blocks)
            ]
        for c in range(blocks):
            member = (zg ^ c) * parts + p
            position = jnp.where(place_ref[3] == 1, blocks * parts - 1 - member, member)
            out_ref[position] = level[c].astype(jnp.bfloat16)


def exchange(pieces, axis, route):
    count = lax.axis_size(axis)
    came = {}
    for offset in sorted(pieces, key=lambda k: abs(k - count // 2)):
        pairs = [(i, route(i, offset) % count) for i in range(count)]
        came[offset] = lax.ppermute(pieces[offset], axis, pairs)
    return [came[offset] for offset in sorted(pieces)]


def body(forward_samples, adjoint_samples, probe_values, owners, block_ranks, twiddle):
    groups, parts = lax.axis_size("zg"), lax.axis_size("smp")
    y_count = lax.axis_size("y")
    samples, points = forward_samples.shape
    vectors = probe_values.shape[1]
    members = groups * parts
    piece = points // members
    smp = lax.axis_index("smp")
    y, core = lax.axis_index("y"), lax.axis_index("core")

    pieces = forward_samples.reshape(samples, members, piece).transpose(1, 0, 2)
    own, probes = owners.T, probe_values.T
    rows = (own, adjoint_samples, probes)
    came = [lax.ppermute(x, "core", [(0, 1), (1, 0)]) for x in rows]
    pieces, *came = lax.optimization_barrier((pieces, *came))
    rows = (own, adjoint_samples, probes, *came)
    pieces = lax.all_to_all(pieces, GROUP, 0, 0, tiled=True)

    place = jnp.stack([y, core])
    shape = (lax.axis_size(Z_AXES), samples * vectors // 128, 128)
    sums = {}
    for offset in sorted(range(y_count), key=lambda k: (k == 0, abs(k - y_count // 2))):
        value = local_call(
            lambda *refs, offset=offset: partial_kernel(y_count, offset, *refs),
            jax.ShapeDtypeStruct(shape, jnp.bfloat16 if offset else jnp.float32),
            place,
            *rows,
            smem=1,
            scratch=[pltpu.VMEM((shape[0] * samples, own.shape[1]), jnp.bfloat16)],
            flops=16 * shape[0] * samples * own.shape[1] * 256,
        )
        route = [(i, (i + offset) % y_count) for i in range(y_count)]
        sums[offset] = lax.ppermute(value, "y", route) if offset else value
    sums = [sums[offset] for offset in range(y_count)]
    shape = (groups,) + shape[1:]
    shapes = [jax.ShapeDtypeStruct(shape, jnp.float32), jax.ShapeDtypeStruct(shape, jnp.bfloat16)]
    zl = lax.axis_index("zl")
    kept, sent = local_call(halve_kernel, shapes, zl[None], *sums, smem=1)
    came = lax.ppermute(sent, "zl", [(0, 1), (1, 0)])
    tail = 8 * piece // shape[2]
    shapes = [jax.ShapeDtypeStruct(shape, jnp.float32)]
    shapes += [jax.ShapeDtypeStruct((tail, shape[2]), jnp.bfloat16)]
    offer = (groups * shape[1] + tail, shape[2])
    shapes += [jax.ShapeDtypeStruct(offer, jnp.bfloat16)] * (groups - 1)
    zg = lax.axis_index("zg")
    place = jnp.stack([zg, smp, block_ranks[0], core])
    partial, extra, *offers = local_call(
        offer_kernel,
        shapes,
        place,
        kept,
        came,
        twiddle,
        smem=1,
        scratch=[pltpu.VMEM(shape, jnp.float32)],
    )
    *offers, pieces = lax.optimization_barrier((*offers, pieces))
    offers = exchange(dict(enumerate(offers, 1)), "zg", lambda i, k: i ^ k)
    shapes = [jax.ShapeDtypeStruct(shape, jnp.bfloat16)]
    shapes += [jax.ShapeDtypeStruct((groups,) + extra.shape, jnp.bfloat16)]
    weights, factors = local_call(
        weights_kernel,
        shapes,
        place,
        partial,
        extra,
        *offers,
        smem=1,
    )
    others = exchange({p: weights for p in range(1, parts)}, "smp", lambda i, k: i + k)
    result = local_call(
        lambda *refs: field_kernel(groups, parts, *refs),
        jax.ShapeDtypeStruct((members, vectors // parts, piece), jnp.bfloat16),
        place,
        pieces,
        factors,
        weights,
        *others,
        smem=1,
        scratch=[
            pltpu.VMEM((groups, vectors, piece), jnp.float32),
            pltpu.VMEM((parts,) + shape, jnp.bfloat16),
        ],
        flops=2 * members * samples * vectors * piece,
    )
    axes = BLK + ("smp",)
    lists = reversed_groups(*(lax.axis_size(axis) for axis in axes))
    result = lax.all_to_all(result, axes, 0, 0, tiled=True, axis_index_groups=lists)
    return join(place, result)


def solution(mesh):
    grid = Mesh(mesh.devices.reshape(4, 2, 4, 2, 4), BLK + ("smp",))
    in_specs = (
        P("smp", BLK),
        P("smp", BLK),
        P(BLK, None),
        P(BLK, None),
        P(BLK),
        P(None, BLK),
    )
    out_specs = P("smp", BLK)
    return jax.shard_map(body, mesh=grid, in_specs=in_specs, out_specs=out_specs, check_vma=False)
```

```python
import jax
import jax.numpy as jnp
from jax import lax
from jax.experimental import pallas as pl
from jax.experimental.pallas import tpu as pltpu
from jax.sharding import Mesh, PartitionSpec as P

GROUP = ("zg", "smp")
Z_AXES = ("zg", "zl")
BLK = ("zg", "zl", "y", "core")
MIB = 1024 * 1024
VMEM = pl.BlockSpec(memory_space=pltpu.VMEM)
SMEM = pl.BlockSpec(memory_space=pltpu.SMEM)


def partial_kernel(y_count, offset, place_ref, *refs):
    out_ref, masked = refs[-2:]
    z_count = out_ref.shape[0]
    y = lax.rem(place_ref[0] + offset, y_count)
    product = None
    for owners_ref, adjoint_ref, probes_ref in (refs[0:3], refs[3:6]):
        own = owners_ref[...]
        adjoint = adjoint_ref[...]
        samples = adjoint.shape[0]
        for z in range(z_count):
            owner = (z * y_count + y) * 2 + place_ref[1]
            hot = jnp.where(own == owner, 1.0, 0.0).astype(jnp.bfloat16)
            masked[z * samples:(z + 1) * samples, :] = adjoint * hot
        term = lax.dot_general(
            masked[...],
            probes_ref[...],
            (((1,), (1,)), ((), ())),
            preferred_element_type=jnp.float32,
        )
        product = term if product is None else product + term
    half = samples // 2
    for z in range(z_count):
        block = product[z * samples:(z + 1) * samples, :]
        tail = jnp.concatenate([block[:half, 128:], block[half:, 128:]], axis=1)
        out_ref[z, :samples, :] = block[:, :128].astype(out_ref.dtype)
        out_ref[z, samples:, :] = tail.astype(out_ref.dtype)


def local_call(kernel, out_shape, *args, smem=0, scratch=(), flops=0, moved=2 * MIB):
    return pl.pallas_call(
        kernel,
        out_shape=out_shape,
        in_specs=[SMEM] * smem + [VMEM] * (len(args) - smem),
        out_specs=jax.tree.map(lambda _: VMEM, out_shape),
        scratch_shapes=list(scratch),
        compiler_params=pltpu.CompilerParams(vmem_limit_bytes=12 * MIB),
        cost_estimate=pl.CostEstimate(flops=flops, bytes_accessed=moved, transcendentals=0),
    )(*args)


def place_of(member, count, core):
    return jnp.where(core == 1, count - 1 - member, member)


def reversed_groups(zg, zl, y, core, smp):
    groups = []
    for rest in range(zl * y * core):
        members = [((g * zl * y * core) + rest) * smp + p for g in range(zg) for p in range(smp)]
        groups.append(members[::-1] if rest % core else members)
    return groups


def halve_kernel(place_ref, *refs):
    kept_ref, sent_ref = refs[-2:]
    for block in range(kept_ref.shape[0]):
        for parity, out_ref in ((place_ref[0], kept_ref), (1 - place_ref[0], sent_ref)):
            z = block * 2 + parity
            total = refs[0][z]
            for ref in refs[1:-2]:
                total = total + ref[z].astype(jnp.float32)
            out_ref[block] = total.astype(out_ref.dtype)


def offer_kernel(place_ref, kept_ref, came_ref, twiddle_ref, own_ref, extra_ref, *refs):
    out_refs, total = refs[:-1], refs[-1]
    zg, smp, rank = place_ref[0], place_ref[1], place_ref[2]
    blocks, packed, lanes = kept_ref.shape
    levels, points = twiddle_ref.shape
    piece = points // (blocks * blocks)
    total[...] = kept_ref[...] + came_ref[...].astype(jnp.float32)
    rank = jnp.full((8 - 3 * levels, lanes), rank.astype(jnp.float32))
    for distance in range(blocks):
        partner = zg ^ distance
        start = place_of(partner * blocks + smp, blocks * blocks, place_ref[3]) * piece
        rows = []
        for column in range(piece // lanes):
            left = twiddle_ref[:, pl.ds(pl.multiple_of(start + column * lanes, lanes), lanes)]
            for _ in range(3):
                term = left.astype(jnp.bfloat16).astype(jnp.float32)
                left = left - term
                rows.append(term)
            rows.append(rank)
        rows = jnp.concatenate(rows, axis=0).astype(jnp.bfloat16)
        for block in range(blocks):
            value = total[partner ^ block]
            if distance == 0:
                own_ref[block] = value
            else:
                target = slice(block * packed, (block + 1) * packed)
                out_refs[distance - 1][target, :] = value.astype(jnp.bfloat16)
        if distance == 0:
            extra_ref[...] = rows
        else:
            out_refs[distance - 1][blocks * packed:, :] = rows


def weights_kernel(place_ref, own_ref, extra_ref, *refs):
    offers, (out_ref, rows_ref) = refs[:-2], refs[-2:]
    blocks, packed, lanes = own_ref.shape
    samples = packed * 2 // 3
    row = lax.broadcasted_iota(jnp.int32, (packed, lanes), 0)
    lane = lax.broadcasted_iota(jnp.int32, (packed, lanes), 1)
    tail = row - samples + jnp.where(lane < 64, 0, samples // 2)
    sample = place_ref[1] * samples + jnp.where(row < samples, row, tail)
    sample = sample.astype(jnp.float32)
    for block in range(blocks):
        total = own_ref[block]
        for offer in offers:
            total = total + offer[block * packed:(block + 1) * packed, :].astype(jnp.float32)
        extra = offers[block - 1][blocks * packed:, :] if block else extra_ref[...]
        rows_ref[block] = extra
        rank = extra.astype(jnp.float32)[6:7]
        out_ref[block] = jnp.where(sample < rank, total, 0.0).astype(jnp.bfloat16)


def field_kernel(blocks, parts, place_ref, samples_ref, rows_ref, *refs):
    weight_refs = refs[:-3]
    out_ref, field, every = refs[-3:]
    zg, smp = place_ref[0], place_ref[1]
    vectors, points = field.shape[1:]
    samples = samples_ref.shape[1]
    for p in range(parts):
        every[place_of(lax.rem(smp - p + parts, parts), parts, place_ref[3])] = weight_refs[p][...]
    factors = []
    for c in range(blocks):
        head, tail, columns = [], [], []
        for p in range(parts):
            head.append(every[p, c, :samples, :])
            rest = every[p, c, samples:, :]
            tail += [rest[:, :64], rest[:, 64:]]
        extra = rows_ref[c].astype(jnp.float32)
        for column in range(extra.shape[0] // 8):
            terms = extra[column * 8:column * 8 + 8]
            columns.append(terms[0:2] + terms[2:4] + terms[4:6])
        factors.append(jnp.concatenate(columns, axis=1))
        first = place_of(zg ^ c, blocks, place_ref[3]) * parts
        grid = samples_ref[pl.ds(first, parts)].reshape(parts * samples, points)
        head = jnp.concatenate(head, axis=0)
        tail = jnp.concatenate(tail, axis=0)
        field[c, :128, :] = lax.dot_general(
            head, grid, (((0,), (0,)), ((), ())), preferred_element_type=jnp.float32
        )
        field[c, 128:, :] = lax.dot_general(
            tail, grid, (((0,), (0,)), ((), ())), preferred_element_type=jnp.float32
        )
    share = vectors // parts
    for p in range(parts):
        rows = slice(p * share, (p + 1) * share)
        level = [field[c, rows, :] for c in range(blocks)]
        for index, distance in enumerate((2, 1)):
            level = [
                level[c] + factors[c][index:index + 1, :] * level[c ^ distance]
                for c in range(blocks)
            ]
        for c in range(blocks):
            target = place_of((zg ^ c) * parts + p, blocks * parts, place_ref[3])
            out_ref[target] = level[c].astype(jnp.bfloat16)


def exchange(pieces, axis, route):
    count = lax.axis_size(axis)
    came = {}
    for offset in sorted(pieces, key=lambda k: abs(k - count // 2)):
        pairs = [(i, route(i, offset) % count) for i in range(count)]
        came[offset] = lax.ppermute(pieces[offset], axis, pairs)
    return [came[offset] for offset in sorted(pieces)]


def body(forward_samples, adjoint_samples, probe_values, owners, block_ranks, twiddle):
    groups, parts = lax.axis_size("zg"), lax.axis_size("smp")
    y_count = lax.axis_size("y")
    samples, points = forward_samples.shape
    vectors = probe_values.shape[1]
    members = groups * parts
    piece = points // members
    smp = lax.axis_index("smp")
    y, core = lax.axis_index("y"), lax.axis_index("core")

    pieces = forward_samples.reshape(samples, members, piece).transpose(1, 0, 2)
    own, probes = owners.T, probe_values.T
    rows = (own, adjoint_samples, probes)
    came = [lax.ppermute(x, "core", [(0, 1), (1, 0)]) for x in rows]
    pieces, *came = lax.optimization_barrier((pieces, *came))
    rows = (own, adjoint_samples, probes, *came)
    axes = BLK + ("smp",)
    lists = reversed_groups(*(lax.axis_size(axis) for axis in axes))
    pieces = lax.all_to_all(pieces, axes, 0, 0, tiled=True, axis_index_groups=lists)

    place = jnp.stack([y, core])
    shape = (lax.axis_size(Z_AXES), samples * vectors // 128, 128)
    sums = {}
    for offset in sorted(range(y_count), key=lambda k: (k == 0, abs(k - y_count // 2))):
        value = local_call(
            lambda *refs, offset=offset: partial_kernel(y_count, offset, *refs),
            jax.ShapeDtypeStruct(shape, jnp.bfloat16 if offset else jnp.float32),
            place,
            *rows,
            smem=1,
            scratch=[pltpu.VMEM((shape[0] * samples, own.shape[1]), jnp.bfloat16)],
            flops=16 * shape[0] * samples * own.shape[1] * 256,
        )
        route = [(i, (i + offset) % y_count) for i in range(y_count)]
        sums[offset] = lax.ppermute(value, "y", route) if offset else value
    sums = [sums[offset] for offset in range(y_count)]
    shape = (groups,) + shape[1:]
    shapes = [jax.ShapeDtypeStruct(shape, jnp.float32), jax.ShapeDtypeStruct(shape, jnp.bfloat16)]
    zl = lax.axis_index("zl")
    kept, sent = local_call(halve_kernel, shapes, zl[None], *sums, smem=1)
    came = lax.ppermute(sent, "zl", [(0, 1), (1, 0)])
    tail = 8 * piece // shape[2]
    shapes = [jax.ShapeDtypeStruct(shape, jnp.float32)]
    shapes += [jax.ShapeDtypeStruct((tail, shape[2]), jnp.bfloat16)]
    offer = (groups * shape[1] + tail, shape[2])
    shapes += [jax.ShapeDtypeStruct(offer, jnp.bfloat16)] * (groups - 1)
    zg = lax.axis_index("zg")
    place = jnp.stack([zg, smp, block_ranks[0], core])
    partial, extra, *offers = local_call(
        offer_kernel,
        shapes,
        place,
        kept,
        came,
        twiddle,
        smem=1,
        scratch=[pltpu.VMEM(shape, jnp.float32)],
    )
    *offers, pieces = lax.optimization_barrier((*offers, pieces))
    offers = exchange(dict(enumerate(offers, 1)), "zg", lambda i, k: i ^ k)
    shapes = [jax.ShapeDtypeStruct(shape, jnp.bfloat16)]
    shapes += [jax.ShapeDtypeStruct((groups,) + extra.shape, jnp.bfloat16)]
    weights, factors = local_call(
        weights_kernel,
        shapes,
        place,
        partial,
        extra,
        *offers,
        smem=1,
    )
    others = exchange({p: weights for p in range(1, parts)}, "smp", lambda i, k: i + k)
    result = local_call(
        lambda *refs: field_kernel(groups, parts, *refs),
        jax.ShapeDtypeStruct((members, vectors // parts, piece), jnp.bfloat16),
        place,
        pieces,
        factors,
        weights,
        *others,
        smem=1,
        scratch=[
            pltpu.VMEM((groups, vectors, piece), jnp.float32),
            pltpu.VMEM((parts,) + shape, jnp.bfloat16),
        ],
        flops=2 * members * samples * vectors * piece,
    )
    result = lax.all_to_all(result, axes, 0, 0, tiled=True, axis_index_groups=lists)
    return result.transpose(1, 0, 2).reshape(vectors // parts, points)


def solution(mesh):
    grid = Mesh(mesh.devices.reshape(4, 2, 4, 2, 4), BLK + ("smp",))
    in_specs = (
        P("smp", BLK),
        P("smp", BLK),
        P(BLK, None),
        P(BLK, None),
        P(BLK),
        P(None, BLK),
    )
    out_specs = P("smp", BLK)
    return jax.shard_map(body, mesh=grid, in_specs=in_specs, out_specs=out_specs, check_vma=False)
```

```python
import jax
import jax.numpy as jnp
from jax import lax
from jax.experimental import pallas as pl
from jax.experimental.pallas import tpu as pltpu
from jax.sharding import Mesh, PartitionSpec as P

GROUP = ("zg", "smp")
Z_AXES = ("zg", "zl")
BLK = ("zg", "zl", "y", "core")
MIB = 1024 * 1024
VMEM = pl.BlockSpec(memory_space=pltpu.VMEM)
SMEM = pl.BlockSpec(memory_space=pltpu.SMEM)


def partial_kernel(y_count, offset, place_ref, *refs):
    out_ref, masked = refs[-2:]
    z_count = out_ref.shape[0]
    y = lax.rem(place_ref[0] + offset, y_count)
    product = None
    for owners_ref, adjoint_ref, probes_ref in (refs[0:3], refs[3:6]):
        own = owners_ref[...]
        adjoint = adjoint_ref[...]
        samples = adjoint.shape[0]
        for z in range(z_count):
            owner = (z * y_count + y) * 2 + place_ref[1]
            hot = jnp.where(own == owner, 1.0, 0.0).astype(jnp.bfloat16)
            masked[z * samples:(z + 1) * samples, :] = adjoint * hot
        term = lax.dot_general(
            masked[...],
            probes_ref[...],
            (((1,), (1,)), ((), ())),
            preferred_element_type=jnp.float32,
        )
        product = term if product is None else product + term
    half = samples // 2
    for z in range(z_count):
        block = product[z * samples:(z + 1) * samples, :]
        tail = jnp.concatenate([block[:half, 128:], block[half:, 128:]], axis=1)
        out_ref[z, :samples, :] = block[:, :128].astype(out_ref.dtype)
        out_ref[z, samples:, :] = tail.astype(out_ref.dtype)


def local_call(kernel, out_shape, *args, smem=0, scratch=(), flops=0, moved=2 * MIB):
    return pl.pallas_call(
        kernel,
        out_shape=out_shape,
        in_specs=[SMEM] * smem + [VMEM] * (len(args) - smem),
        out_specs=jax.tree.map(lambda _: VMEM, out_shape),
        scratch_shapes=list(scratch),
        compiler_params=pltpu.CompilerParams(vmem_limit_bytes=12 * MIB),
        cost_estimate=pl.CostEstimate(flops=flops, bytes_accessed=moved, transcendentals=0),
    )(*args)


def place_of(member, count, core):
    return jnp.where(core == 1, count - 1 - member, member)


def reversed_groups(zg, zl, y, core, smp):
    groups = []
    for rest in range(zl * y * core):
        members = [((g * zl * y * core) + rest) * smp + p for g in range(zg) for p in range(smp)]
        groups.append(members[::-1] if rest % core else members)
    return groups


def halve_kernel(place_ref, *refs):
    kept_ref, sent_ref = refs[-2:]
    for block in range(kept_ref.shape[0]):
        for parity, out_ref in ((place_ref[0], kept_ref), (1 - place_ref[0], sent_ref)):
            z = block * 2 + parity
            total = refs[0][z]
            for ref in refs[1:-2]:
                total = total + ref[z].astype(jnp.float32)
            out_ref[block] = total.astype(out_ref.dtype)


def offer_kernel(place_ref, kept_ref, came_ref, twiddle_ref, own_ref, extra_ref, *refs):
    out_refs, total = refs[:-1], refs[-1]
    zg, smp, rank = place_ref[0], place_ref[1], place_ref[2]
    blocks, packed, lanes = kept_ref.shape
    levels, points = twiddle_ref.shape
    piece = points // (blocks * blocks)
    total[...] = kept_ref[...] + came_ref[...].astype(jnp.float32)
    rank = jnp.full((8 - 3 * levels, lanes), rank.astype(jnp.float32))
    for distance in range(blocks):
        partner = zg ^ distance
        start = place_of(partner * blocks + smp, blocks * blocks, place_ref[3]) * piece
        rows = []
        for column in range(piece // lanes):
            left = twiddle_ref[:, pl.ds(pl.multiple_of(start + column * lanes, lanes), lanes)]
            for _ in range(3):
                term = left.astype(jnp.bfloat16).astype(jnp.float32)
                left = left - term
                rows.append(term)
            rows.append(rank)
        rows = jnp.concatenate(rows, axis=0).astype(jnp.bfloat16)
        for block in range(blocks):
            value = total[partner ^ block]
            if distance == 0:
                own_ref[block] = value
            else:
                target = slice(block * packed, (block + 1) * packed)
                out_refs[distance - 1][target, :] = value.astype(jnp.bfloat16)
        if distance == 0:
            extra_ref[...] = rows
        else:
            out_refs[distance - 1][blocks * packed:, :] = rows


def weights_kernel(place_ref, own_ref, extra_ref, *refs):
    offers, (out_ref, rows_ref) = refs[:-2], refs[-2:]
    blocks, packed, lanes = own_ref.shape
    samples = packed * 2 // 3
    row = lax.broadcasted_iota(jnp.int32, (packed, lanes), 0)
    lane = lax.broadcasted_iota(jnp.int32, (packed, lanes), 1)
    tail = row - samples + jnp.where(lane < 64, 0, samples // 2)
    sample = place_ref[1] * samples + jnp.where(row < samples, row, tail)
    sample = sample.astype(jnp.float32)
    for block in range(blocks):
        total = own_ref[block]
        for offer in offers:
            total = total + offer[block * packed:(block + 1) * packed, :].astype(jnp.float32)
        extra = offers[block - 1][blocks * packed:, :] if block else extra_ref[...]
        rows_ref[block] = extra
        rank = extra.astype(jnp.float32)[6:7]
        weights = jnp.where(sample < rank, total, 0.0).astype(jnp.bfloat16)
        for part in range(out_ref.shape[0]):
            out_ref[part, block] = weights


def field_kernel(blocks, parts, place_ref, samples_ref, rows_ref, weights_ref, *refs):
    out_ref, field, every = refs
    zg = place_ref[0]
    vectors, points = field.shape[1:]
    samples = samples_ref.shape[1]
    for p in range(parts):
        every[place_of(p, parts, place_ref[3])] = weights_ref[p]
    factors = []
    for c in range(blocks):
        head, tail, columns = [], [], []
        for p in range(parts):
            head.append(every[p, c, :samples, :])
            rest = every[p, c, samples:, :]
            tail += [rest[:, :64], rest[:, 64:]]
        extra = rows_ref[c].astype(jnp.float32)
        for column in range(extra.shape[0] // 8):
            terms = extra[column * 8:column * 8 + 8]
            columns.append(terms[0:2] + terms[2:4] + terms[4:6])
        factors.append(jnp.concatenate(columns, axis=1))
        first = place_of(zg ^ c, blocks, place_ref[3]) * parts
        grid = samples_ref[pl.ds(first, parts)].reshape(parts * samples, points)
        head = jnp.concatenate(head, axis=0)
        tail = jnp.concatenate(tail, axis=0)
        field[c, :128, :] = lax.dot_general(
            head, grid, (((0,), (0,)), ((), ())), preferred_element_type=jnp.float32
        )
        field[c, 128:, :] = lax.dot_general(
            tail, grid, (((0,), (0,)), ((), ())), preferred_element_type=jnp.float32
        )
    share = vectors // parts
    for p in range(parts):
        rows = slice(p * share, (p + 1) * share)
        level = [field[c, rows, :] for c in range(blocks)]
        for index, distance in enumerate((2, 1)):
            level = [
                level[c] + factors[c][index:index + 1, :] * level[c ^ distance]
                for c in range(blocks)
            ]
        for c in range(blocks):
            target = place_of((zg ^ c) * parts + p, blocks * parts, place_ref[3])
            out_ref[target] = level[c].astype(jnp.bfloat16)


def exchange(pieces, axis, route):
    count = lax.axis_size(axis)
    came = {}
    for offset in sorted(pieces, key=lambda k: abs(k - count // 2)):
        pairs = [(i, route(i, offset) % count) for i in range(count)]
        came[offset] = lax.ppermute(pieces[offset], axis, pairs)
    return [came[offset] for offset in sorted(pieces)]


def body(forward_samples, adjoint_samples, probe_values, owners, block_ranks, twiddle):
    groups, parts = lax.axis_size("zg"), lax.axis_size("smp")
    y_count = lax.axis_size("y")
    samples, points = forward_samples.shape
    vectors = probe_values.shape[1]
    members = groups * parts
    piece = points // members
    smp = lax.axis_index("smp")
    y, core = lax.axis_index("y"), lax.axis_index("core")

    pieces = forward_samples.reshape(samples, members, piece).transpose(1, 0, 2)
    own, probes = owners.T, probe_values.T
    rows = (own, adjoint_samples, probes)
    came = [lax.ppermute(x, "core", [(0, 1), (1, 0)]) for x in rows]
    pieces, *came = lax.optimization_barrier((pieces, *came))
    rows = (own, adjoint_samples, probes, *came)
    axes = BLK + ("smp",)
    lists = reversed_groups(*(lax.axis_size(axis) for axis in axes))
    pieces = lax.all_to_all(pieces, axes, 0, 0, tiled=True, axis_index_groups=lists)

    place = jnp.stack([y, core])
    shape = (lax.axis_size(Z_AXES), samples * vectors // 128, 128)
    sums = {}
    for offset in sorted(range(y_count), key=lambda k: (k == 0, abs(k - y_count // 2))):
        value = local_call(
            lambda *refs, offset=offset: partial_kernel(y_count, offset, *refs),
            jax.ShapeDtypeStruct(shape, jnp.bfloat16 if offset else jnp.float32),
            place,
            *rows,
            smem=1,
            scratch=[pltpu.VMEM((shape[0] * samples, own.shape[1]), jnp.bfloat16)],
            flops=16 * shape[0] * samples * own.shape[1] * 256,
        )
        route = [(i, (i + offset) % y_count) for i in range(y_count)]
        sums[offset] = lax.ppermute(value, "y", route) if offset else value
    sums = [sums[offset] for offset in range(y_count)]
    shape = (groups,) + shape[1:]
    shapes = [jax.ShapeDtypeStruct(shape, jnp.float32), jax.ShapeDtypeStruct(shape, jnp.bfloat16)]
    zl = lax.axis_index("zl")
    kept, sent = local_call(halve_kernel, shapes, zl[None], *sums, smem=1)
    came = lax.ppermute(sent, "zl", [(0, 1), (1, 0)])
    tail = 8 * piece // shape[2]
    shapes = [jax.ShapeDtypeStruct(shape, jnp.float32)]
    shapes += [jax.ShapeDtypeStruct((tail, shape[2]), jnp.bfloat16)]
    offer = (groups * shape[1] + tail, shape[2])
    shapes += [jax.ShapeDtypeStruct(offer, jnp.bfloat16)] * (groups - 1)
    zg = lax.axis_index("zg")
    place = jnp.stack([zg, smp, block_ranks[0], core])
    partial, extra, *offers = local_call(
        offer_kernel,
        shapes,
        place,
        kept,
        came,
        twiddle,
        smem=1,
        scratch=[pltpu.VMEM(shape, jnp.float32)],
    )
    *offers, pieces = lax.optimization_barrier((*offers, pieces))
    offers = exchange(dict(enumerate(offers, 1)), "zg", lambda i, k: i ^ k)
    shapes = [jax.ShapeDtypeStruct((parts,) + shape, jnp.bfloat16)]
    shapes += [jax.ShapeDtypeStruct((groups,) + extra.shape, jnp.bfloat16)]
    weights, factors = local_call(
        weights_kernel,
        shapes,
        place,
        partial,
        extra,
        *offers,
        smem=1,
    )
    weights = lax.all_to_all(weights, "smp", 0, 0, tiled=True)
    result = local_call(
        lambda *refs: field_kernel(groups, parts, *refs),
        jax.ShapeDtypeStruct((members, vectors // parts, piece), jnp.bfloat16),
        place,
        pieces,
        factors,
        weights,
        smem=1,
        scratch=[
            pltpu.VMEM((groups, vectors, piece), jnp.float32),
            pltpu.VMEM((parts,) + shape, jnp.bfloat16),
        ],
        flops=2 * members * samples * vectors * piece,
    )
    result = lax.all_to_all(result, axes, 0, 0, tiled=True, axis_index_groups=lists)
    return result.transpose(1, 0, 2).reshape(vectors // parts, points)


def solution(mesh):
    grid = Mesh(mesh.devices.reshape(4, 2, 4, 2, 4), BLK + ("smp",))
    in_specs = (
        P("smp", BLK),
        P("smp", BLK),
        P(BLK, None),
        P(BLK, None),
        P(BLK),
        P(None, BLK),
    )
    out_specs = P("smp", BLK)
    return jax.shard_map(body, mesh=grid, in_specs=in_specs, out_specs=out_specs, check_vma=False)
```

```python
import jax
import jax.numpy as jnp
from jax import lax
from jax.experimental import pallas as pl
from jax.experimental.pallas import tpu as pltpu
from jax.sharding import Mesh, PartitionSpec as P

GROUP = ("zg", "smp")
Z_AXES = ("zg", "zl")
BLK = ("zg", "zl", "y", "core")
MIB = 1024 * 1024
VMEM = pl.BlockSpec(memory_space=pltpu.VMEM)
SMEM = pl.BlockSpec(memory_space=pltpu.SMEM)


def split_kernel(source_ref, out_ref, sems):
    pieces, _, points = out_ref.shape
    copies = [
        pltpu.make_async_copy(source_ref.at[:, pl.ds(i * points, points)], out_ref.at[i], sems.at[i])
        for i in range(pieces)
    ]
    for copy in copies:
        copy.start()
    for copy in copies:
        copy.wait()


def split(source, pieces):
    rows, points = source.shape
    return pl.pallas_call(
        split_kernel,
        out_shape=jax.ShapeDtypeStruct((pieces, rows, points // pieces), source.dtype),
        in_specs=[pl.BlockSpec(memory_space=pl.ANY)],
        out_specs=VMEM,
        scratch_shapes=[pltpu.SemaphoreType.DMA((pieces,))],
        compiler_params=pltpu.CompilerParams(vmem_limit_bytes=56 * MIB),
        cost_estimate=pl.CostEstimate(flops=0, bytes_accessed=2 * MIB, transcendentals=0),
    )(source)


def partial_kernel(y_count, offset, other, place_ref, owners_ref, adjoint_ref, wide_ref, *refs):
    out_ref, masked = refs[-2:]
    samples = adjoint_ref.shape[0]
    z_count = out_ref.shape[0]
    own = owners_ref[...]
    adjoint = adjoint_ref[...]
    y = lax.rem(place_ref[0] + offset, y_count)
    core = 1 - place_ref[1] if other else place_ref[1]
    for z in range(z_count):
        hot = jnp.where(own == (z * y_count + y) * 2 + core, 1.0, 0.0).astype(jnp.bfloat16)
        masked[z * samples:(z + 1) * samples, :] = adjoint * hot
    product = lax.dot_general(
        masked[...], wide_ref[...], (((1,), (1,)), ((), ())), preferred_element_type=jnp.float32
    )
    half = samples // 2
    low = lax.broadcasted_iota(jnp.int32, (half, 128), 1) < 64
    for z in range(z_count):
        block = product[z * samples:(z + 1) * samples, :]
        head = block[:, :128]
        tail = jnp.where(low, block[:half, 128:], block[half:, 128:])
        if not other:
            head = head + refs[0][z, :samples, :]
            tail = tail + refs[0][z, samples:, :]
        out_ref[z, :samples, :] = head.astype(out_ref.dtype)
        out_ref[z, samples:, :] = tail.astype(out_ref.dtype)


def local_call(kernel, out_shape, *args, smem=0, scratch=(), flops=0):
    return pl.pallas_call(
        kernel,
        out_shape=out_shape,
        in_specs=[SMEM] * smem + [VMEM] * (len(args) - smem),
        out_specs=jax.tree.map(lambda _: VMEM, out_shape),
        scratch_shapes=list(scratch),
        compiler_params=pltpu.CompilerParams(vmem_limit_bytes=12 * MIB),
        cost_estimate=pl.CostEstimate(flops=flops, bytes_accessed=2 * MIB, transcendentals=0),
    )(*args)


def halve_kernel(place_ref, *refs):
    kept_ref, sent_ref = refs[-2:]
    for block in range(kept_ref.shape[0]):
        for parity, out_ref in ((place_ref[0], kept_ref), (1 - place_ref[0], sent_ref)):
            z = block * 2 + parity
            total = refs[0][z]
            for ref in refs[1:-2]:
                total = total + ref[z].astype(jnp.float32)
            out_ref[block] = total.astype(out_ref.dtype)


def offer_kernel(place_ref, kept_ref, came_ref, twiddle_ref, own_ref, extra_ref, *refs):
    out_refs, total = refs[:-1], refs[-1]
    zg, smp, rank = place_ref[0], place_ref[1], place_ref[2]
    blocks, packed, lanes = kept_ref.shape
    levels, points = twiddle_ref.shape
    piece = points // (blocks * blocks)
    total[...] = kept_ref[...] + came_ref[...].astype(jnp.float32)
    rank = jnp.full((8 - 3 * levels, lanes), rank.astype(jnp.float32))
    for distance in range(blocks):
        partner = zg ^ distance
        start = (partner * blocks + smp) * piece
        rows = []
        for column in range(piece // lanes):
            left = twiddle_ref[:, pl.ds(pl.multiple_of(start + column * lanes, lanes), lanes)]
            for _ in range(3):
                term = left.astype(jnp.bfloat16).astype(jnp.float32)
                left = left - term
                rows.append(term)
            rows.append(rank)
        rows = jnp.concatenate(rows, axis=0).astype(jnp.bfloat16)
        for block in range(blocks):
            value = total[partner ^ block]
            if distance == 0:
                own_ref[block] = value
            else:
                target = slice(block * packed, (block + 1) * packed)
                out_refs[distance - 1][target, :] = value.astype(jnp.bfloat16)
        if distance == 0:
            extra_ref[...] = rows
        else:
            out_refs[distance - 1][blocks * packed:, :] = rows


def weights_kernel(place_ref, own_ref, extra_ref, *refs):
    offers, out_ref = refs[:-1], refs[-1]
    blocks, packed, lanes = own_ref.shape
    samples = packed * 2 // 3
    row = lax.broadcasted_iota(jnp.int32, (packed, lanes), 0)
    lane = lax.broadcasted_iota(jnp.int32, (packed, lanes), 1)
    tail = row - samples + jnp.where(lane < 64, 0, samples // 2)
    sample = place_ref[1] * samples + jnp.where(row < samples, row, tail)
    sample = sample.astype(jnp.float32)
    for block in range(blocks):
        total = own_ref[block]
        for offer in offers:
            total = total + offer[block * packed:(block + 1) * packed, :].astype(jnp.float32)
        extra = offers[block - 1][blocks * packed:, :] if block else extra_ref[...]
        rank = extra.astype(jnp.float32)[6:7]
        out_ref[block] = jnp.where(sample < rank, total, 0.0).astype(jnp.bfloat16)


def field_kernel(blocks, parts, place_ref, samples_ref, extra_ref, *refs):
    offers, weight_refs = refs[:blocks - 1], refs[blocks - 1:-2]
    out_ref, field = refs[-2:]
    zg, smp = place_ref[0], place_ref[1]
    vectors, points = field.shape[1:]
    samples = samples_ref.shape[1]
    packed = weight_refs[0].shape[1]
    factors = []
    for c in range(blocks):
        head, tail, columns, grid = [], [], [], []
        for p in range(parts):
            grid.append(samples_ref[(zg ^ c) * parts + lax.rem(smp - p + parts, parts)])
            head.append(weight_refs[p][c, :samples, :])
            rest = weight_refs[p][c, samples:, :]
            tail += [rest[:, :64], rest[:, 64:]]
        extra = offers[c - 1][blocks * packed:, :] if c else extra_ref[...]
        extra = extra.astype(jnp.float32)
        for column in range(extra.shape[0] // 8):
            terms = extra[column * 8:column * 8 + 8]
            columns.append(terms[0:2] + terms[2:4] + terms[4:6])
        factors.append(jnp.concatenate(columns, axis=1))
        grid = jnp.concatenate(grid, axis=0)
        head = jnp.concatenate(head, axis=0)
        tail = jnp.concatenate(tail, axis=0)
        field[c, :128, :] = lax.dot_general(
            head, grid, (((0,), (0,)), ((), ())), preferred_element_type=jnp.float32
        )
        field[c, 128:, :] = lax.dot_general(
            tail, grid, (((0,), (0,)), ((), ())), preferred_element_type=jnp.float32
        )
    share = vectors // parts
    for p in range(parts):
        rows = slice(p * share, (p + 1) * share)
        level = [field[c, rows, :] for c in range(blocks)]
        for index, distance in enumerate((2, 1)):
            level = [
                level[c] + factors[c][index:index + 1, :] * level[c ^ distance]
                for c in range(blocks)
            ]
        for c in range(blocks):
            out_ref[(zg ^ c) * parts + p] = level[c].astype(jnp.bfloat16)


def exchange(pieces, axis, route):
    count = lax.axis_size(axis)
    came = {}
    for offset in sorted(pieces, key=lambda k: abs(k - count // 2)):
        pairs = [(i, route(i, offset) % count) for i in range(count)]
        came[offset] = lax.ppermute(pieces[offset], axis, pairs)
    return [came[offset] for offset in sorted(pieces)]


def body(forward_samples, adjoint_samples, probe_values, owners, block_ranks, twiddle):
    groups, parts = lax.axis_size("zg"), lax.axis_size("smp")
    y_count = lax.axis_size("y")
    samples, points = forward_samples.shape
    vectors = probe_values.shape[1]
    members = groups * parts
    piece = points // members
    smp = lax.axis_index("smp")
    y, core = lax.axis_index("y"), lax.axis_index("core")

    pieces = split(forward_samples, members)
    own, probes = owners.T, probe_values.T
    pieces, own = lax.optimization_barrier((pieces, own))
    pieces = lax.all_to_all(pieces, GROUP, 0, 0, tiled=True)

    wide = jnp.concatenate([probes, probes[128:]], axis=0)
    shape = (lax.axis_size(Z_AXES), samples * vectors // 128, 128)
    place = jnp.stack([y, core])

    def partial(offset, other, kind, *came):
        return local_call(
            lambda *refs: partial_kernel(y_count, offset, other, *refs),
            jax.ShapeDtypeStruct(shape, kind),
            place,
            own,
            adjoint_samples,
            wide,
            *came,
            smem=1,
            scratch=[pltpu.VMEM((shape[0] * samples, own.shape[1]), jnp.bfloat16)],
            flops=4 * shape[0] * samples * own.shape[1] * 256,
        )

    order = sorted(range(y_count), key=lambda k: (k == 0, abs(k - y_count // 2)))
    came = {}
    for offset in order:
        sent = partial(offset, True, jnp.float32)
        came[offset] = lax.ppermute(sent, "core", [(0, 1), (1, 0)])
    sums = []
    for offset in order:
        kind = jnp.bfloat16 if offset else jnp.float32
        merged = partial(offset, False, kind, came[offset])
        route = [(i, (i + offset) % y_count) for i in range(y_count)]
        sums.append(lax.ppermute(merged, "y", route) if offset else merged)
    sums = sums[-1:] + sums[:-1]
    shape = (groups,) + shape[1:]
    shapes = [jax.ShapeDtypeStruct(shape, jnp.float32), jax.ShapeDtypeStruct(shape, jnp.bfloat16)]
    zl = lax.axis_index("zl")
    kept, sent = local_call(halve_kernel, shapes, zl[None], *sums, smem=1)
    came = lax.ppermute(sent, "zl", [(0, 1), (1, 0)])
    tail = 8 * piece // shape[2]
    shapes = [jax.ShapeDtypeStruct(shape, jnp.float32)]
    shapes += [jax.ShapeDtypeStruct((tail, shape[2]), jnp.bfloat16)]
    offer = (groups * shape[1] + tail, shape[2])
    shapes += [jax.ShapeDtypeStruct(offer, jnp.bfloat16)] * (groups - 1)
    zg = lax.axis_index("zg")
    place = jnp.stack([zg, smp, block_ranks[0]])
    partial, extra, *offers = local_call(
        offer_kernel,
        shapes,
        place,
        kept,
        came,
        twiddle,
        smem=1,
        scratch=[pltpu.VMEM(shape, jnp.float32)],
    )
    *offers, pieces = lax.optimization_barrier((*offers, pieces))
    offers = exchange(dict(enumerate(offers, 1)), "zg", lambda i, k: i ^ k)
    weights = local_call(
        weights_kernel,
        jax.ShapeDtypeStruct(shape, jnp.bfloat16),
        place,
        partial,
        extra,
        *offers,
        smem=1,
    )
    others = exchange({p: weights for p in range(1, parts)}, "smp", lambda i, k: i + k)
    result = local_call(
        lambda *refs: field_kernel(groups, parts, *refs),
        jax.ShapeDtypeStruct((members, vectors // parts, piece), jnp.bfloat16),
        place,
        pieces,
        extra,
        *offers,
        weights,
        *others,
        smem=1,
        scratch=[pltpu.VMEM((groups, vectors, piece), jnp.float32)],
        flops=2 * members * samples * vectors * piece,
    )
    result = lax.all_to_all(result, GROUP, 0, 0, tiled=True)
    return result.transpose(1, 0, 2).reshape(vectors // parts, points)


def solution(mesh):
    grid = Mesh(mesh.devices.reshape(4, 2, 4, 2, 4), BLK + ("smp",))
    in_specs = (
        P("smp", BLK),
        P("smp", BLK),
        P(BLK, None),
        P(BLK, None),
        P(BLK),
        P(None, BLK),
    )
    out_specs = P("smp", BLK)
    return jax.shard_map(body, mesh=grid, in_specs=in_specs, out_specs=out_specs, check_vma=False)
```
